32 devices in a mesh: src: 16 (over z, x, core), tgt: 2 (over y).
Axes of the slice: x: 2, y: 2, z: 4, core: 2. Of those that a mesh axis runs over, the one named last changes fastest.
Arguments:
- upstream: bfloat16 [128, 128, 324], P('src'), may hold values from -6 to 6
- centers: int32 [2, 128, 128], P(None, 'src'), may hold values from -4 to 259, as said below
- post_relu: bfloat16 [128, 128, 128], P('src'), as said below
- conv_input: bfloat16 [128, 128, 128], P(('src', 'tgt')), may hold values from -6 to 6
- target_feats: bfloat16 [16, 256, 256], P('tgt'), may hold values from -6 to 6
- out_weight: bfloat16 [128, 256], replicated, may hold values from -0.5 to 0.5
- conv_weight: bfloat16 [3, 3, 128, 128], replicated, may hold values from -0.1875 to 0.1875
Outputs:
- tgt_grad: bfloat16 [16, 256, 256], P('tgt', 'src')
- act_grad: bfloat16 [128, 128, 128], P(('src', 'tgt'))
- out_wgrad: float32 [128, 256], replicated
- conv_wgrad: float32 [3, 3, 128, 128], replicated
The draws below stay inside these ranges and needn't reach their ends.
Inputs may be any that keep to these rules, and one draw needn't show every extreme that they name: centers[0] is a target row from -4 to 19 and centers[1] a target column from -4 to 259; windows may reach outside the target image. `post_relu`: entries are zero or positive.
All inputs are finite; a program needn't handle non-finite values.
Results may differ from the reference program's by a relative error of at most 0.0064.
Values may be sent and summed in bfloat16 or wider, within the bound.
A program may use at most 64 MiB of HBM per device.

```python
import math
import jax
import jax.numpy as jnp
from jax import lax

D = 256
CH = 128
WIN = 324
SW = 128
TW = 256
SH = 128
TH = 16


def draw_centers(key, part):
    row_key = jax.random.fold_in(key, 11)
    col_key = jax.random.fold_in(key, 12)
    row_vals = jax.random.randint(row_key, (1, SH, SW), -4, TH + 4, dtype=jnp.int32)
    col_vals = jax.random.randint(col_key, (1, SH, SW), -4, TW + 4, dtype=jnp.int32)
    return jnp.concatenate([row_vals, col_vals], axis=0)


def draw_post_relu(key, part):
    values = jax.random.normal(key, (SH, SW, CH), jnp.float32)
    return jnp.maximum(values, 0.0).astype(jnp.bfloat16)


def shard_levels(stream_key, shape, cuts, low, top_value):
    def one(position, shards_of):
        steps = jax.random.uniform(jax.random.fold_in(jax.random.fold_in(stream_key, 6), position), (shards_of,), jnp.float32, low / len(cuts), top_value / len(cuts))
        return jnp.repeat(jnp.exp(steps), shape[position] // shards_of).reshape((-1,) + (1,) * (len(shape) - position - 1))

    gain = one(*cuts[0])
    for cut in cuts[1:]:
        gain = gain * one(*cut)
    return gain


def centred(key, dims, spread, reach, cuts=(), kind=jnp.bfloat16):
    array = jax.random.normal(key, dims, jnp.float32) * spread
    if len(cuts) > 0:
        array = shard_levels(key, dims, cuts, -0.22, 0.18) * array
    return jnp.clip(array, min=-reach, max=reach).astype(kind)


def setup_inputs(seed: int = 0) -> dict:
    splits = jax.random.split(jax.random.key(seed), 8)
    return {
        "upstream": centred(splits[0], (SH, SW, WIN), 1.0, 6.0, ((0, 16),)),
        "centers": draw_centers(jax.random.fold_in(splits[7], 71), 0),
        "post_relu": draw_post_relu(jax.random.fold_in(splits[7], 71), 0),
        "conv_input": centred(splits[3], (SH, SW, CH), 1.0, 6.0, ((0, 32),)),
        "target_feats": centred(splits[4], (TH, TW, D), 1.0, 6.0, ((0, 2),)),
        "out_weight": centred(splits[5], (CH, D), CH ** -0.5, 0.5),
        "conv_weight": centred(splits[6], (3, 3, CH, CH), (9 * CH) ** -0.5, 0.1875),
    }


def settle(value):
    return lax.optimization_barrier(value).astype(jnp.float32)

def corr_block(center_rows, center_cols, grad_rows, row_start, row_total, col_total):
    source_total = grad_rows.shape[0]
    row_ids = row_start + jnp.arange(row_total, dtype=jnp.int32)
    col_ids = jnp.arange(col_total, dtype=jnp.int32)
    offsets = jnp.arange(9, dtype=jnp.int32)
    row_parts = []
    col_parts = []
    for level_no in range(4):
        level_step = 2 ** level_no
        row_off = jnp.floor_divide(row_ids, level_step)[None, :] - jnp.floor_divide(center_rows, level_step)[:, None] + 4
        col_off = jnp.floor_divide(col_ids, level_step)[None, :] - jnp.floor_divide(center_cols, level_step)[:, None] + 4
        row_hot = jnp.where(row_off[:, None, :] == offsets[None, :, None], 0.25 ** level_no, 0.0).astype(jnp.float32)
        col_hot = jnp.where(col_off[:, None, :] == offsets[None, :, None], 1.0, 0.0).astype(jnp.float32)
        level_grads = grad_rows[:, 81 * level_no:81 * (level_no + 1)].astype(jnp.float32).reshape(source_total, 9, 9)
        row_parts.append(row_hot)
        col_parts.append(jnp.einsum('sab,sbx->sax', level_grads, col_hot))
    row_table = jnp.concatenate(row_parts, axis=1)
    col_table = jnp.concatenate(col_parts, axis=1)
    return jnp.einsum('say,sax->syx', row_table, col_table).astype(jnp.bfloat16)

def reference(upstream, centers, post_relu, conv_input, target_feats, out_weight, conv_weight):
    source_total = SH * SW
    flat_grads = upstream.reshape(source_total, WIN)
    flat_rows = centers[0].reshape(source_total)
    flat_cols = centers[1].reshape(source_total)
    relu_flat = post_relu.reshape(source_total, CH).astype(jnp.float32)
    src_feats = jnp.dot(relu_flat, out_weight.astype(jnp.float32), preferred_element_type=jnp.float32).astype(jnp.bfloat16)
    feats_f = settle(src_feats)
    flat_targets = target_feats.reshape(TH * TW, D).astype(jnp.float32)
    block_size = 4 * SW
    inv_root = 1.0 / math.sqrt(D)

    def accumulate(target_acc, block_no):
        first_row = block_no * block_size
        corr_rows = corr_block(lax.dynamic_slice_in_dim(flat_rows, first_row, block_size), lax.dynamic_slice_in_dim(flat_cols, first_row, block_size), lax.dynamic_slice_in_dim(flat_grads, first_row, block_size, 0), jnp.int32(0), TH, TW)
        corr_rows = settle(corr_rows.reshape(block_size, TH * TW))
        feat_rows = lax.dynamic_slice_in_dim(feats_f, first_row, block_size, 0)
        src_part = jnp.dot(corr_rows, flat_targets, preferred_element_type=jnp.float32) * inv_root
        return (target_acc + jnp.dot(corr_rows.T, feat_rows, preferred_element_type=jnp.float32), src_part)
    target_acc, src_parts = lax.scan(accumulate, jnp.zeros((TH * TW, D), jnp.float32), jnp.arange(SH // 4, dtype=jnp.int32))
    tgt_grad = (target_acc * inv_root).reshape(TH, TW, D).astype(jnp.bfloat16)
    src_grad = src_parts.reshape(SH, SW, D).astype(jnp.bfloat16)
    grad_f = settle(src_grad).reshape(source_total, D)
    out_wgrad = jnp.dot(relu_flat.T, grad_f, preferred_element_type=jnp.float32) / SH
    hidden = jnp.dot(grad_f, out_weight.astype(jnp.float32).T, preferred_element_type=jnp.float32).reshape(SH, SW, CH)
    block_grad = jnp.where(post_relu > 0, hidden, 0.0).astype(jnp.bfloat16)
    padded = jnp.pad(settle(block_grad), ((1, 1), (1, 1), (0, 0)))
    conv_f = conv_weight.astype(jnp.float32)
    input_f = conv_input.astype(jnp.float32)
    act_sum = jnp.zeros((SH, SW, CH), jnp.float32)
    tap_grads = []
    for row_tap in range(3):
        for col_tap in range(3):
            window = padded[2 - row_tap:2 - row_tap + SH, 2 - col_tap:2 - col_tap + SW]
            act_sum = act_sum + jnp.einsum('rwo,io->rwi', window, conv_f[row_tap, col_tap])
            tap_grads.append(jnp.einsum('rwi,rwo->io', input_f, window))
    conv_wgrad = jnp.stack(tap_grads).reshape(3, 3, CH, CH) / SH
    return (tgt_grad, act_sum.astype(jnp.bfloat16), out_wgrad, conv_wgrad)
```

```python
import math

import jax
import jax.numpy as jnp
from jax import lax
from jax.experimental import pallas as pl
from jax.experimental.pallas import tpu as pltpu
from jax.sharding import PartitionSpec as P

OFFSET = (0, 81, 34, 115)
EMPTY = (100, 178, 120, 208)
FAR = 4096


def dot(a, b, dims=((1,), (0,))):
    return lax.dot_general(a, b, (dims, ((), ())), preferred_element_type=jnp.float32)


def spread_matrix(half, width, transposed):
    shape = (384, width) if transposed else (width, 384)
    cell = lax.broadcasted_iota(jnp.int32, shape, 0 if transposed else 1)
    col = lax.broadcasted_iota(jnp.int32, shape, 1 if transposed else 0)
    one = jnp.where(cell == (col >> 1), 0.25, 0.0)
    two = jnp.where(cell == 128 + 64 * half + (col >> 2), 0.0625, 0.0)
    three = jnp.where(cell == 256 + (col >> 3), 0.015625, 0.0)
    return (one + two + three).astype(jnp.bfloat16)


def build_table(row_first, up_ref, cen_ref, rows_ref, cols_ref, tail_ref, table_ref):
    total = up_ref.shape[0]
    for r in range(total // 128):
        for part, ref in ((0, rows_ref), (1, cols_ref)):
            line = jnp.broadcast_to(cen_ref[part, r : r + 1, :], (128, 128))
            ref[r * 128 : (r + 1) * 128, :] = jnp.transpose(line)
    tail_ref[:, 0:68] = up_ref[:, 256:324].astype(jnp.float32)
    lane = lax.broadcasted_iota(jnp.int32, (16, 128), 1)

    @pl.loop(0, total // 16)
    def _(group):
        here = pl.ds(pl.multiple_of(group * 16, 16), 16)
        first = up_ref[here, 0:128].astype(jnp.float32)
        second = up_ref[here, 128:256].astype(jnp.float32)
        third = tail_ref[here, :]
        source = (
            jnp.where(lane < 81, first, 0.0),
            jnp.where(lane >= 81, first, jnp.where(lane < 34, second, 0.0)),
            jnp.where((lane >= 34) & (lane < 115), second, 0.0),
            jnp.where(lane >= 115, second, jnp.where(lane < 68, third, 0.0)),
        )
        center_row = rows_ref[here, :]
        center_col = cols_ref[here, :]

        def row_term(level, cell):
            a = cell + ((row_first >> level) + 4) - (center_row >> level)
            return jnp.where((a >= 0) & (a < 9), 9 * a + OFFSET[level], FAR)

        def col_term(level, cell):
            b = cell + 4 - (center_col >> level)
            return jnp.where((b >= 0) & (b < 9), b, FAR)

        def put(level, tile, index):
            index = jnp.minimum(index, EMPTY[level]) & 127
            value = jnp.take_along_axis(source[level], index, axis=1, mode="promise_in_bounds")
            table_ref[here, tile * 128 : (tile + 1) * 128] = value.astype(jnp.bfloat16)

        halves = [col_term(0, lane + 128 * h) for h in range(2)]
        for y in range(8):
            a = row_term(0, y)
            for h in range(2):
                put(0, 2 * y + h, a + halves[h])
        b = col_term(1, lane)
        for j in range(4):
            put(1, 16 + j, row_term(1, j) + b)
        put(2, 20, row_term(2, lane >> 6) + col_term(2, lane & 63))
        put(3, 21, jnp.where(lane < 32, row_term(3, 0) + col_term(3, lane), FAR))


def corr_kernel(
    up_ref, cen_ref, relu_ref, tf_ref, ow_ref,
    src_ref, tgt_ref,
    rows_ref, cols_ref, tail_ref, table_ref, pooled_ref, sums_ref, feats_ref,
):
    total = up_ref.shape[0]
    width = tf_ref.shape[1]
    feat = tf_ref.shape[2]
    dense = tf_ref.shape[0] * width
    scale = 1.0 / math.sqrt(feat)
    row_first = lax.axis_index("tgt") * tf_ref.shape[0]
    build_table(row_first, up_ref, cen_ref, rows_ref, cols_ref, tail_ref, table_ref)

    mats = [spread_matrix(half, width, True) for half in range(2)]
    coarse = jnp.zeros((256, feat), jnp.float32)
    for j in range(4):
        fine = jnp.zeros((128, feat), jnp.float32)
        for y in (2 * j, 2 * j + 1):
            part = dot(mats[y // 4], tf_ref[y])
            fine = fine + part[:128]
            coarse = coarse + part[128:]
        pooled_ref[j * 128 : (j + 1) * 128, :] = fine.astype(jnp.bfloat16)
    pooled_ref[512:768, :] = coarse.astype(jnp.bfloat16)

    feats_ref[...] = dot(ow_ref[...], relu_ref[...], ((0,), (1,))).astype(jnp.bfloat16)

    @pl.loop(0, total // 256)
    def _(block):
        here = pl.ds(pl.multiple_of(block * 256, 256), 256)
        value = dot(table_ref[here, :dense], tf_ref[...].reshape(dense, feat))
        value = value + dot(table_ref[here, dense:], pooled_ref[...])
        src_ref[here, :] = (value * scale).astype(src_ref.dtype)

    @pl.loop(0, table_ref.shape[1] // 256)
    def _(tile):
        here = pl.ds(pl.multiple_of(tile * 256, 256), 256)
        sums_ref[:, here] = dot(feats_ref[...], table_ref[:, here]).astype(jnp.bfloat16)

    eye = (
        lax.broadcasted_iota(jnp.int32, (width, width), 0)
        == lax.broadcasted_iota(jnp.int32, (width, width), 1)
    )
    eye = jnp.where(eye, 1.0, 0.0).astype(jnp.bfloat16)
    for y in range(8):
        mat = spread_matrix(y // 4, width, False)
        j = y // 2
        value = dot(eye, sums_ref[:, y * 256 : (y + 1) * 256], ((1,), (1,)))
        value = value + dot(
            mat[:, :128], sums_ref[:, dense + j * 128 : dense + (j + 1) * 128], ((1,), (1,))
        )
        value = value + dot(mat[:, 128:], sums_ref[:, dense + 512 :], ((1,), (1,)))
        tgt_ref[y] = (value * scale).astype(tgt_ref.dtype)


def corr_grads(upstream, centers, post_relu, target_feats, out_weight):
    total = upstream.shape[0] * upstream.shape[1]
    rows, width, feat = target_feats.shape
    assert rows == 8 and width == 256
    cells = rows * width + 768
    vmem = pl.BlockSpec(memory_space=pltpu.VMEM)
    return pl.pallas_call(
        corr_kernel,
        out_shape=(
            jax.ShapeDtypeStruct((total, feat), jnp.float32),
            jax.ShapeDtypeStruct((rows, width, feat), jnp.float32),
        ),
        in_specs=[vmem] * 5,
        out_specs=(vmem, vmem),
        scratch_shapes=[
            pltpu.VMEM((total, 128), jnp.int32),
            pltpu.VMEM((total, 128), jnp.int32),
            pltpu.VMEM((total, 128), jnp.float32),
            pltpu.VMEM((total, cells), jnp.bfloat16),
            pltpu.VMEM((768, feat), jnp.bfloat16),
            pltpu.VMEM((feat, cells), jnp.bfloat16),
            pltpu.VMEM((feat, total), jnp.bfloat16),
        ],
        compiler_params=pltpu.CompilerParams(vmem_limit_bytes=48 * 2**20),
        cost_estimate=pl.CostEstimate(
            flops=4 * total * cells * feat, bytes_accessed=6 * 2**20, transcendentals=0
        ),
    )(
        upstream.reshape(total, -1),
        centers,
        post_relu.reshape(total, -1),
        target_feats,
        out_weight,
    )


def padded_2(array, sides, width):
    for axis, dim in sides:
        devices, length = (lax.axis_size(axis), array.shape[dim])
        up = [(i, (i + 1) % devices) for i in range(devices - 1)]
        down = [(j, i) for i, j in up]
        last = lax.slice_in_dim(array, length - width, length, axis=dim)
        first = lax.slice_in_dim(array, 0, width, axis=dim)
        before = lax.ppermute(last, axis, up)
        after = lax.ppermute(first, axis, down)
        array = jnp.concatenate([before, array, after], axis=dim)
    return array


def hidden_grads(src_grad, relu_rows, out_weight):
    hidden = jnp.einsum("rwd,cd->rwc", src_grad, out_weight, preferred_element_type=jnp.float32)
    block_grad = jnp.where(relu_rows > 0, hidden, 0.0).astype(jnp.bfloat16)
    out_term = jnp.einsum("rwc,rwd->cd", relu_rows, src_grad, preferred_element_type=jnp.float32)
    return (block_grad, out_term)


def conv_back(grad_pad, inputs, kernel):
    row_total = inputs.shape[0]
    width_total = inputs.shape[1]
    padded = jnp.pad(grad_pad, ((0, 0), (1, 1), (0, 0)))
    act_sum = jnp.zeros(inputs.shape, jnp.float32)
    tap_grads = []
    for row_tap in range(3):
        for col_tap in range(3):
            window = padded[
                2 - row_tap : 2 - row_tap + row_total, 2 - col_tap : 2 - col_tap + width_total
            ]
            act_sum = act_sum + jnp.einsum(
                "rwo,io->rwi", window, kernel[row_tap, col_tap], preferred_element_type=jnp.float32
            )
            tap_grads.append(
                jnp.einsum("rwi,rwo->io", inputs, window, preferred_element_type=jnp.float32)
            )
    channels = inputs.shape[2]
    return (act_sum, jnp.stack(tap_grads).reshape(3, 3, channels, channels))


def body(upstream, centers, post_relu, conv_input, target_feats, out_weight, conv_weight):
    src_rows, src_width, lookups = upstream.shape
    feat_width = target_feats.shape[2]
    src_devices = lax.axis_size("src")
    tgt_devices = lax.axis_size("tgt")
    product, target = corr_grads(upstream, centers, post_relu, target_feats, out_weight)
    target_share = lax.psum_scatter(target, "src", scatter_dimension=1, tiled=True)
    tgt_grad = target_share.astype(jnp.bfloat16)
    tile_rows = src_rows // tgt_devices
    src_grad = lax.psum_scatter(
        product.reshape(src_rows, src_width, feat_width),
        "tgt",
        scatter_dimension=0,
        tiled=True,
    ).astype(jnp.bfloat16)
    relu_tile = lax.dynamic_slice_in_dim(post_relu, lax.axis_index("tgt") * tile_rows, tile_rows, 0)
    block_grad, out_term = hidden_grads(src_grad, relu_tile, out_weight)
    grad_pad = padded_2(block_grad, ((("src", "tgt"), 0),), 1)
    act_sum, conv_term = conv_back(grad_pad, conv_input, conv_weight)
    out_total, conv_total = lax.psum((out_term, conv_term), ("src", "tgt"))
    act_grad = act_sum.astype(jnp.bfloat16)
    row_count = float(src_rows * src_devices)
    return (tgt_grad, act_grad, out_total / row_count, conv_total / row_count)


def solution(mesh):
    placed = (
        P("src", None, None),
        P(None, "src", None),
        P("src", None, None),
        P(("src", "tgt"), None, None),
        P("tgt", None, None),
        P(),
        P(),
    )
    return jax.shard_map(
        body,
        mesh=mesh,
        in_specs=placed,
        out_specs=(P("tgt", "src", None), P(("src", "tgt"), None, None), P(), P()),
        check_vma=False,
    )
```

```python
import math

import jax
import jax.numpy as jnp
from jax import lax
from jax.experimental import pallas as pl
from jax.experimental.pallas import tpu as pltpu
from jax.sharding import PartitionSpec as P

OFFSET = (0, 81, 34, 115)
EMPTY = (100, 178, 120, 208)
FAR = 4096
PIECES = 2
MESH = pl.DeviceIdType.MESH


def dot(a, b, dims=((1,), (0,))):
    return lax.dot_general(a, b, (dims, ((), ())), preferred_element_type=jnp.float32)


def spread_matrix(half, width, transposed):
    shape = (384, width) if transposed else (width, 384)
    cell = lax.broadcasted_iota(jnp.int32, shape, 0 if transposed else 1)
    col = lax.broadcasted_iota(jnp.int32, shape, 1 if transposed else 0)
    one = jnp.where(cell == (col >> 1), 0.25, 0.0)
    two = jnp.where(cell == 128 + 64 * half + (col >> 2), 0.0625, 0.0)
    three = jnp.where(cell == 256 + (col >> 3), 0.015625, 0.0)
    return (one + two + three).astype(jnp.bfloat16)


def build_table(row_first, up_ref, cen_ref, rows_ref, cols_ref, tail_ref, table_ref):
    total = up_ref.shape[0]
    for r in range(total // 128):
        for part, ref in ((0, rows_ref), (1, cols_ref)):
            line = jnp.broadcast_to(cen_ref[part, r : r + 1, :], (128, 128))
            ref[r * 128 : (r + 1) * 128, :] = jnp.transpose(line)
    tail_ref[:, 0:68] = up_ref[:, 256:324].astype(jnp.float32)
    lane = lax.broadcasted_iota(jnp.int32, (16, 128), 1)

    @pl.loop(0, total // 16)
    def _(group):
        here = pl.ds(pl.multiple_of(group * 16, 16), 16)
        first = up_ref[here, 0:128].astype(jnp.float32)
        second = up_ref[here, 128:256].astype(jnp.float32)
        third = tail_ref[here, :]
        source = (
            jnp.where(lane < 81, first, 0.0),
            jnp.where(lane >= 81, first, jnp.where(lane < 34, second, 0.0)),
            jnp.where((lane >= 34) & (lane < 115), second, 0.0),
            jnp.where(lane >= 115, second, jnp.where(lane < 68, third, 0.0)),
        )
        center_row = rows_ref[here, :]
        center_col = cols_ref[here, :]

        def row_term(level, cell):
            a = cell + ((row_first >> level) + 4) - (center_row >> level)
            return jnp.where((a >= 0) & (a < 9), 9 * a + OFFSET[level], FAR)

        def col_term(level, cell):
            b = cell + 4 - (center_col >> level)
            return jnp.where((b >= 0) & (b < 9), b, FAR)

        def put(level, tile, index):
            index = jnp.minimum(index, EMPTY[level]) & 127
            value = jnp.take_along_axis(source[level], index, axis=1, mode="promise_in_bounds")
            table_ref[here, tile * 128 : (tile + 1) * 128] = value.astype(jnp.bfloat16)

        halves = [col_term(0, lane + 128 * h) for h in range(2)]
        for y in range(8):
            a = row_term(0, y)
            for h in range(2):
                put(0, 2 * y + h, a + halves[h])
        b = col_term(1, lane)
        for j in range(4):
            put(1, 16 + j, row_term(1, j) + b)
        put(2, 20, row_term(2, lane >> 6) + col_term(2, lane & 63))
        put(3, 21, jnp.where(lane < 32, row_term(3, 0) + col_term(3, lane), FAR))


def corr_kernel(
    up_ref, cen_ref, relu_ref, tf_ref, ow_ref,
    src_ref, tgt_ref,
    rows_ref, cols_ref, tail_ref, table_ref, pooled_ref, sums_ref, feats_ref,
):
    total = up_ref.shape[0]
    width = tf_ref.shape[1]
    feat = tf_ref.shape[2]
    dense = tf_ref.shape[0] * width
    scale = 1.0 / math.sqrt(feat)
    row_first = lax.axis_index("tgt") * tf_ref.shape[0]
    build_table(row_first, up_ref, cen_ref, rows_ref, cols_ref, tail_ref, table_ref)

    mats = [spread_matrix(half, width, True) for half in range(2)]
    coarse = jnp.zeros((256, feat), jnp.float32)
    for j in range(4):
        fine = jnp.zeros((128, feat), jnp.float32)
        for y in (2 * j, 2 * j + 1):
            part = dot(mats[y // 4], tf_ref[y])
            fine = fine + part[:128]
            coarse = coarse + part[128:]
        pooled_ref[j * 128 : (j + 1) * 128, :] = fine.astype(jnp.bfloat16)
    pooled_ref[512:768, :] = coarse.astype(jnp.bfloat16)

    feats_ref[...] = dot(ow_ref[...], relu_ref[...], ((0,), (1,))).astype(jnp.bfloat16)

    @pl.loop(0, total // 256)
    def _(block):
        here = pl.ds(pl.multiple_of(block * 256, 256), 256)
        value = dot(table_ref[here, :dense], tf_ref[...].reshape(dense, feat))
        value = value + dot(table_ref[here, dense:], pooled_ref[...])
        src_ref[here, :] = (value * scale).astype(src_ref.dtype)

    @pl.loop(0, table_ref.shape[1] // 256)
    def _(tile):
        here = pl.ds(pl.multiple_of(tile * 256, 256), 256)
        sums_ref[:, here] = dot(feats_ref[...], table_ref[:, here]).astype(jnp.bfloat16)

    eye = (
        lax.broadcasted_iota(jnp.int32, (width, width), 0)
        == lax.broadcasted_iota(jnp.int32, (width, width), 1)
    )
    eye = jnp.where(eye, 1.0, 0.0).astype(jnp.bfloat16)
    for y in range(8):
        mat = spread_matrix(y // 4, width, False)
        j = y // 2
        value = dot(eye, sums_ref[:, y * 256 : (y + 1) * 256], ((1,), (1,)))
        value = value + dot(
            mat[:, :128], sums_ref[:, dense + j * 128 : dense + (j + 1) * 128], ((1,), (1,))
        )
        value = value + dot(mat[:, 128:], sums_ref[:, dense + 512 :], ((1,), (1,)))
        value = (value * scale).astype(tgt_ref.dtype)
        pieces, _, _, groups, lines, share, _ = tgt_ref.shape
        for k in range(4 * groups):
            tgt_ref[y // lines, k % 2, k // 2 % 2, k // 4, y % lines] = value[
                k * share : (k + 1) * share
            ]


def corr_grads(upstream, centers, post_relu, target_feats, out_weight, devices):
    total = upstream.shape[0] * upstream.shape[1]
    rows, width, feat = target_feats.shape
    assert rows == 8 and width == 256
    cells = rows * width + 768
    vmem = pl.BlockSpec(memory_space=pltpu.VMEM)
    return pl.pallas_call(
        corr_kernel,
        out_shape=(
            jax.ShapeDtypeStruct((total, feat), jnp.bfloat16),
            jax.ShapeDtypeStruct(
                (PIECES, 2, 2, devices // 4, rows // PIECES, width // devices, feat), jnp.bfloat16
            ),
        ),
        in_specs=[vmem] * 5,
        out_specs=(vmem, vmem),
        scratch_shapes=[
            pltpu.VMEM((total, 128), jnp.int32),
            pltpu.VMEM((total, 128), jnp.int32),
            pltpu.VMEM((total, 128), jnp.float32),
            pltpu.VMEM((total, cells), jnp.bfloat16),
            pltpu.VMEM((768, feat), jnp.bfloat16),
            pltpu.VMEM((feat, cells), jnp.bfloat16),
            pltpu.VMEM((feat, total), jnp.bfloat16),
        ],
        compiler_params=pltpu.CompilerParams(vmem_limit_bytes=48 * 2**20),
        cost_estimate=pl.CostEstimate(
            flops=4 * total * cells * feat, bytes_accessed=6 * 2**20, transcendentals=0
        ),
    )(
        upstream.reshape(total, -1),
        centers,
        post_relu.reshape(total, -1),
        target_feats,
        out_weight,
    )


def shift(value, step, size):
    return lax.rem(value + step, size)


def exchange_kernel(
    devices, teams, prod_ref, part_ref, src_ref, tgt_ref,
    got_core, got_pair, got_far, got_src, sum_core, sum_pair,
    core_send, core_recv, pair_send, pair_recv, far_send, far_recv, src_send, src_recv,
):
    s = lax.axis_index("src")
    t = lax.axis_index("tgt")
    groups = devices // 4
    core, pair, far = lax.rem(s, 2), lax.rem(s // 2, 2), s // 4
    core_mate = (s + 1 - 2 * core, t)
    pair_mate = (s + 2 - 4 * pair, t)

    def far_mate(d):
        return (shift(far, d, groups) * 4 + pair * 2 + core, t)

    mates = [core_mate, pair_mate]
    mates += [far_mate(d) for d in range(1, groups)]
    mates += [(s, shift(t, d, teams)) for d in range(1, teams)]
    barrier = pltpu.get_barrier_semaphore()
    for mate in mates:
        pl.semaphore_signal(barrier, inc=1, device_id=mate, device_id_type=MESH)
    pl.semaphore_wait(barrier, len(mates))

    def send(src, dst, send_sem, recv_sem, mate):
        copy = pltpu.make_async_remote_copy(
            src_ref=src, dst_ref=dst, send_sem=send_sem, recv_sem=recv_sem,
            device_id=mate, device_id_type=MESH,
        )
        copy.start()
        return copy

    core_copies = [
        send(part_ref.at[q, 1 - core], got_core.at[q], core_send.at[q], core_recv.at[q], core_mate)
        for q in range(PIECES)
    ]
    src_copies = [
        send(
            prod_ref.at[shift(t, d, teams)], got_src.at[d - 1],
            src_send.at[d - 1], src_recv.at[d - 1], (s, shift(t, d, teams)),
        )
        for d in range(1, teams)
    ]
    pair_copies = []
    for q in range(PIECES):
        core_copies[q].wait()
        for half in range(2):
            value = part_ref[q, core, half].astype(jnp.float32)
            value = value + got_core[q, half].astype(jnp.float32)
            sum_core[q, half] = value.astype(jnp.bfloat16)
        pair_copies.append(
            send(sum_core.at[q, 1 - pair], got_pair.at[q], pair_send.at[q], pair_recv.at[q], pair_mate)
        )
    far_copies = []
    for q in range(PIECES):
        pair_copies[q].wait()
        value = sum_core[q, pair].astype(jnp.float32) + got_pair[q].astype(jnp.float32)
        sum_pair[q] = value.astype(jnp.bfloat16)
        far_copies.append([
            send(
                sum_pair.at[q, shift(far, d, groups)], got_far.at[q, d - 1],
                far_send.at[q, d - 1], far_recv.at[q, d - 1], far_mate(d),
            )
            for d in range(1, groups)
        ])
    for copy in src_copies:
        copy.wait()
    value = prod_ref[t].astype(jnp.float32)
    for d in range(1, teams):
        value = value + got_src[d - 1].astype(jnp.float32)
    src_ref[...] = value.astype(jnp.bfloat16)
    lines = part_ref.shape[4]
    for q in range(PIECES):
        value = sum_pair[q, far].astype(jnp.float32)
        for d in range(1, groups):
            far_copies[q][d - 1].wait()
            value = value + got_far[q, d - 1].astype(jnp.float32)
        tgt_ref[q * lines : (q + 1) * lines] = value.astype(jnp.bfloat16)


def exchange(product, part, devices, teams):
    total, feat = product.shape
    tile = total // teams
    _, _, _, groups, lines, share, _ = part.shape
    vmem = pl.BlockSpec(memory_space=pltpu.VMEM)
    block = (groups, lines, share, feat)
    dma = pltpu.SemaphoreType.DMA
    return pl.pallas_call(
        lambda *refs: exchange_kernel(devices, teams, *refs),
        out_shape=(
            jax.ShapeDtypeStruct((tile, feat), jnp.bfloat16),
            jax.ShapeDtypeStruct((PIECES * lines, share, feat), jnp.bfloat16),
        ),
        in_specs=[vmem] * 2,
        out_specs=(vmem, vmem),
        scratch_shapes=[
            pltpu.VMEM((PIECES, 2) + block, jnp.bfloat16),
            pltpu.VMEM((PIECES,) + block, jnp.bfloat16),
            pltpu.VMEM((PIECES,) + block, jnp.bfloat16),
            pltpu.VMEM((teams, tile, feat), jnp.bfloat16),
            pltpu.VMEM((PIECES, 2) + block, jnp.bfloat16),
            pltpu.VMEM((PIECES,) + block, jnp.bfloat16),
            dma((PIECES,)), dma((PIECES,)), dma((PIECES,)), dma((PIECES,)),
            dma((PIECES, groups)), dma((PIECES, groups)),
            dma((teams,)), dma((teams,)),
        ],
        compiler_params=pltpu.CompilerParams(
            collective_id=0, has_side_effects=True, vmem_limit_bytes=32 * 2**20
        ),
    )(product.reshape(teams, tile, feat), part)


def total_kernel(
    teams, count, term_ref, out_ref, got_core, got_far, held, full,
    core_send, core_recv, far_send, far_recv, all_send, all_recv, last_send, last_recv,
):
    s = lax.axis_index("src")
    t = lax.axis_index("tgt")
    size = term_ref.shape[1]
    core = lax.rem(s, 2)
    me = (s // 2) * teams + t
    mate = (s + 1 - 2 * core, t)

    def place(rank):
        return (rank // teams * 2 + core, lax.rem(rank, teams))

    barrier = pltpu.get_barrier_semaphore()
    pl.semaphore_signal(barrier, inc=1, device_id=mate, device_id_type=MESH)

    @pl.loop(1, size)
    def _(d):
        pl.semaphore_signal(
            barrier, inc=1, device_id=place(shift(me, d, size)), device_id_type=MESH
        )

    pl.semaphore_wait(barrier, size)

    def remote(src, dst, send_sem, recv_sem, device):
        return pltpu.make_async_remote_copy(
            src_ref=src, dst_ref=dst, send_sem=send_sem, recv_sem=recv_sem,
            device_id=device, device_id_type=MESH,
        )

    copy = remote(term_ref.at[1 - core], got_core, core_send, core_recv, mate)
    copy.start()
    copy.wait()
    value = term_ref[core].astype(jnp.float32) + got_core[...].astype(jnp.float32)
    held[...] = value.astype(jnp.bfloat16)

    def far_copy(d):
        rank = shift(me, d, size)
        return remote(
            held.at[rank], got_far.at[d - 1], far_send.at[d - 1], far_recv.at[d - 1], place(rank)
        )

    @pl.loop(1, size)
    def _(d):
        far_copy(d).start()

    def add(d, value):
        far_copy(d).wait()
        return value + got_far[d - 1].astype(jnp.float32)

    value = lax.fori_loop(1, size, add, held[me].astype(jnp.float32))
    full[core, me] = value.astype(jnp.bfloat16)

    def all_copy(d, rank):
        return remote(
            full.at[core, rank], full.at[core, rank],
            all_send.at[d - 1], all_recv.at[d - 1], place(shift(me, d, size)),
        )

    @pl.loop(1, size)
    def _(d):
        all_copy(d, me).start()

    @pl.loop(1, size)
    def _(d):
        all_copy(d, me).wait_send()
        all_copy(d, shift(me, size - d, size)).wait_recv()

    remote(full.at[core], full.at[core], last_send, last_recv, mate).start()
    remote(full.at[core], full.at[core], last_send, last_recv, mate).wait_send()
    remote(full.at[1 - core], full.at[1 - core], last_send, last_recv, mate).wait_recv()
    out_ref[...] = full[...].astype(jnp.float32) * (1.0 / count)


def weight_totals(out_term, conv_term, devices, teams, count):
    size = devices * teams // 2
    flat = jnp.concatenate([out_term.reshape(-1, 128), conv_term.reshape(-1, 128)], axis=0)
    flat = flat.astype(jnp.bfloat16)
    used = flat.shape[0]
    lines = -(-used // (2 * size * 16)) * 16
    flat = jnp.pad(flat, ((0, 2 * size * lines - used), (0, 0)))
    vmem = pl.BlockSpec(memory_space=pltpu.VMEM)
    dma = pltpu.SemaphoreType.DMA
    full = pl.pallas_call(
        lambda *refs: total_kernel(teams, count, *refs),
        out_shape=jax.ShapeDtypeStruct((2, size, lines, 128), jnp.float32),
        in_specs=[vmem],
        out_specs=vmem,
        scratch_shapes=[
            pltpu.VMEM((size, lines, 128), jnp.bfloat16),
            pltpu.VMEM((size, lines, 128), jnp.bfloat16),
            pltpu.VMEM((size, lines, 128), jnp.bfloat16),
            pltpu.VMEM((2, size, lines, 128), jnp.bfloat16),
            dma, dma, dma((size,)), dma((size,)), dma((size,)), dma((size,)), dma, dma,
        ],
        compiler_params=pltpu.CompilerParams(
            collective_id=1, has_side_effects=True, vmem_limit_bytes=32 * 2**20
        ),
    )(flat.reshape(2, size, lines, 128))
    full = full.reshape(-1, 128)
    split = out_term.size // 128
    return (
        full[:split].reshape(out_term.shape),
        full[split:used].reshape(conv_term.shape),
    )


def padded_2(array, sides, width):
    for axis, dim in sides:
        devices, length = (lax.axis_size(axis), array.shape[dim])
        up = [(i, (i + 1) % devices) for i in range(devices - 1)]
        down = [(j, i) for i, j in up]
        last = lax.slice_in_dim(array, length - width, length, axis=dim)
        first = lax.slice_in_dim(array, 0, width, axis=dim)
        before = lax.ppermute(last, axis, up)
        after = lax.ppermute(first, axis, down)
        array = jnp.concatenate([before, array, after], axis=dim)
    return array


def hidden_grads(src_grad, relu_rows, out_weight):
    hidden = jnp.einsum("rwd,cd->rwc", src_grad, out_weight, preferred_element_type=jnp.float32)
    block_grad = jnp.where(relu_rows > 0, hidden, 0.0).astype(jnp.bfloat16)
    out_term = jnp.einsum("rwc,rwd->cd", relu_rows, src_grad, preferred_element_type=jnp.float32)
    return (block_grad, out_term)


def conv_back(grad_pad, inputs, kernel):
    row_total = inputs.shape[0]
    width_total = inputs.shape[1]
    padded = jnp.pad(grad_pad, ((0, 0), (1, 1), (0, 0)))
    act_sum = jnp.zeros(inputs.shape, jnp.float32)
    tap_grads = []
    for row_tap in range(3):
        for col_tap in range(3):
            window = padded[
                2 - row_tap : 2 - row_tap + row_total, 2 - col_tap : 2 - col_tap + width_total
            ]
            act_sum = act_sum + jnp.einsum(
                "rwo,io->rwi", window, kernel[row_tap, col_tap], preferred_element_type=jnp.float32
            )
            tap_grads.append(
                jnp.einsum("rwi,rwo->io", inputs, window, preferred_element_type=jnp.float32)
            )
    channels = inputs.shape[2]
    return (act_sum, jnp.stack(tap_grads).reshape(3, 3, channels, channels))


def body(upstream, centers, post_relu, conv_input, target_feats, out_weight, conv_weight):
    src_rows, src_width, lookups = upstream.shape
    feat_width = target_feats.shape[2]
    src_devices = lax.axis_size("src")
    tgt_devices = lax.axis_size("tgt")
    product, part = corr_grads(
        upstream, centers, post_relu, target_feats, out_weight, src_devices
    )
    src_grad, tgt_grad = exchange(product, part, src_devices, tgt_devices)
    tile_rows = src_rows // tgt_devices
    src_grad = src_grad.reshape(tile_rows, src_width, feat_width)
    relu_tile = lax.dynamic_slice_in_dim(post_relu, lax.axis_index("tgt") * tile_rows, tile_rows, 0)
    block_grad, out_term = hidden_grads(src_grad, relu_tile, out_weight)
    grad_pad = padded_2(block_grad, ((("src", "tgt"), 0),), 1)
    act_sum, conv_term = conv_back(grad_pad, conv_input, conv_weight)
    row_count = float(src_rows * src_devices)
    out_total, conv_total = weight_totals(out_term, conv_term, src_devices, tgt_devices, row_count)
    return (tgt_grad, act_sum.astype(jnp.bfloat16), out_total, conv_total)


def solution(mesh):
    placed = (
        P("src", None, None),
        P(None, "src", None),
        P("src", None, None),
        P(("src", "tgt"), None, None),
        P("tgt", None, None),
        P(),
        P(),
    )
    return jax.shard_map(
        body,
        mesh=mesh,
        in_specs=placed,
        out_specs=(P("tgt", "src", None), P(("src", "tgt"), None, None), P(), P()),
        check_vma=False,
    )
```

```python
import math

import jax
import jax.numpy as jnp
from jax import lax
from jax.experimental import pallas as pl
from jax.experimental.pallas import tpu as pltpu
from jax.sharding import PartitionSpec as P

OFFSET = (0, 81, 34, 115)
EMPTY = (100, 178, 120, 208)
FAR = 4096
PIECES = 2
MESH = pl.DeviceIdType.MESH


def dot(a, b, dims=((1,), (0,))):
    return lax.dot_general(a, b, (dims, ((), ())), preferred_element_type=jnp.float32)


def spread_matrix(half, width, transposed):
    shape = (384, width) if transposed else (width, 384)
    cell = lax.broadcasted_iota(jnp.int32, shape, 0 if transposed else 1)
    col = lax.broadcasted_iota(jnp.int32, shape, 1 if transposed else 0)
    one = jnp.where(cell == (col >> 1), 0.25, 0.0)
    two = jnp.where(cell == 128 + 64 * half + (col >> 2), 0.0625, 0.0)
    three = jnp.where(cell == 256 + (col >> 3), 0.015625, 0.0)
    return (one + two + three).astype(jnp.bfloat16)


def build_table(row_first, up_ref, cen_ref, rows_ref, cols_ref, tail_ref, table_ref):
    total = up_ref.shape[0]
    for r in range(total // 128):
        for part, ref in ((0, rows_ref), (1, cols_ref)):
            line = jnp.broadcast_to(cen_ref[part, r : r + 1, :], (128, 128))
            ref[r * 128 : (r + 1) * 128, :] = jnp.transpose(line)
    tail_ref[:, 0:68] = up_ref[:, 256:324].astype(jnp.float32)
    lane = lax.broadcasted_iota(jnp.int32, (16, 128), 1)

    @pl.loop(0, total // 16)
    def _(group):
        here = pl.ds(pl.multiple_of(group * 16, 16), 16)
        first = up_ref[here, 0:128].astype(jnp.float32)
        second = up_ref[here, 128:256].astype(jnp.float32)
        third = tail_ref[here, :]
        source = (
            jnp.where(lane < 81, first, 0.0),
            jnp.where(lane >= 81, first, jnp.where(lane < 34, second, 0.0)),
            jnp.where((lane >= 34) & (lane < 115), second, 0.0),
            jnp.where(lane >= 115, second, jnp.where(lane < 68, third, 0.0)),
        )
        center_row = rows_ref[here, :]
        center_col = cols_ref[here, :]

        def row_term(level, cell):
            a = cell + ((row_first >> level) + 4) - (center_row >> level)
            return jnp.where((a >= 0) & (a < 9), 9 * a + OFFSET[level], FAR)

        def col_term(level, cell):
            b = cell + 4 - (center_col >> level)
            return jnp.where((b >= 0) & (b < 9), b, FAR)

        def put(level, tile, index):
            index = jnp.minimum(index, EMPTY[level]) & 127
            value = jnp.take_along_axis(source[level], index, axis=1, mode="promise_in_bounds")
            table_ref[here, tile * 128 : (tile + 1) * 128] = value.astype(jnp.bfloat16)

        halves = [col_term(0, lane + 128 * h) for h in range(2)]
        for y in range(8):
            a = row_term(0, y)
            for h in range(2):
                put(0, 2 * y + h, a + halves[h])
        b = col_term(1, lane)
        for j in range(4):
            put(1, 16 + j, row_term(1, j) + b)
        put(2, 20, row_term(2, lane >> 6) + col_term(2, lane & 63))
        put(3, 21, jnp.where(lane < 32, row_term(3, 0) + col_term(3, lane), FAR))


def corr_kernel(
    up_ref, cen_ref, relu_ref, tf_ref, ow_ref,
    src_ref, tgt_ref,
    rows_ref, cols_ref, tail_ref, table_ref, pooled_ref, sums_ref, feats_ref,
):
    total = up_ref.shape[0]
    width = tf_ref.shape[1]
    feat = tf_ref.shape[2]
    dense = tf_ref.shape[0] * width
    scale = 1.0 / math.sqrt(feat)
    row_first = lax.axis_index("tgt") * tf_ref.shape[0]
    build_table(row_first, up_ref, cen_ref, rows_ref, cols_ref, tail_ref, table_ref)

    mats = [spread_matrix(half, width, True) for half in range(2)]
    coarse = jnp.zeros((256, feat), jnp.float32)
    for j in range(4):
        fine = jnp.zeros((128, feat), jnp.float32)
        for y in (2 * j, 2 * j + 1):
            part = dot(mats[y // 4], tf_ref[y])
            fine = fine + part[:128]
            coarse = coarse + part[128:]
        pooled_ref[j * 128 : (j + 1) * 128, :] = fine.astype(jnp.bfloat16)
    pooled_ref[512:768, :] = coarse.astype(jnp.bfloat16)

    feats_ref[...] = dot(ow_ref[...], relu_ref[...], ((0,), (1,))).astype(jnp.bfloat16)

    @pl.loop(0, total // 256)
    def _(block):
        here = pl.ds(pl.multiple_of(block * 256, 256), 256)
        value = dot(table_ref[here, :dense], tf_ref[...].reshape(dense, feat))
        value = value + dot(table_ref[here, dense:], pooled_ref[...])
        src_ref[here, :] = (value * scale).astype(src_ref.dtype)

    @pl.loop(0, table_ref.shape[1] // 256)
    def _(tile):
        here = pl.ds(pl.multiple_of(tile * 256, 256), 256)
        sums_ref[:, here] = dot(feats_ref[...], table_ref[:, here]).astype(jnp.bfloat16)

    eye = (
        lax.broadcasted_iota(jnp.int32, (width, width), 0)
        == lax.broadcasted_iota(jnp.int32, (width, width), 1)
    )
    eye = jnp.where(eye, 1.0, 0.0).astype(jnp.bfloat16)
    for y in range(8):
        mat = spread_matrix(y // 4, width, False)
        j = y // 2
        value = dot(eye, sums_ref[:, y * 256 : (y + 1) * 256], ((1,), (1,)))
        value = value + dot(
            mat[:, :128], sums_ref[:, dense + j * 128 : dense + (j + 1) * 128], ((1,), (1,))
        )
        value = value + dot(mat[:, 128:], sums_ref[:, dense + 512 :], ((1,), (1,)))
        value = (value * scale).astype(tgt_ref.dtype)
        pieces, _, _, groups, lines, share, _ = tgt_ref.shape
        for k in range(4 * groups):
            tgt_ref[y // lines, k % 2, k // 2 % 2, k // 4, y % lines] = value[
                k * share : (k + 1) * share
            ]


def corr_grads(upstream, centers, post_relu, target_feats, out_weight, devices):
    total = upstream.shape[0] * upstream.shape[1]
    rows, width, feat = target_feats.shape
    assert rows == 8 and width == 256
    cells = rows * width + 768
    vmem = pl.BlockSpec(memory_space=pltpu.VMEM)
    return pl.pallas_call(
        corr_kernel,
        out_shape=(
            jax.ShapeDtypeStruct((total, feat), jnp.bfloat16),
            jax.ShapeDtypeStruct(
                (PIECES, 2, 2, devices // 4, rows // PIECES, width // devices, feat), jnp.bfloat16
            ),
        ),
        in_specs=[vmem] * 5,
        out_specs=(vmem, vmem),
        scratch_shapes=[
            pltpu.VMEM((total, 128), jnp.int32),
            pltpu.VMEM((total, 128), jnp.int32),
            pltpu.VMEM((total, 128), jnp.float32),
            pltpu.VMEM((total, cells), jnp.bfloat16),
            pltpu.VMEM((768, feat), jnp.bfloat16),
            pltpu.VMEM((feat, cells), jnp.bfloat16),
            pltpu.VMEM((feat, total), jnp.bfloat16),
        ],
        compiler_params=pltpu.CompilerParams(vmem_limit_bytes=48 * 2**20),
        cost_estimate=pl.CostEstimate(
            flops=4 * total * cells * feat, bytes_accessed=6 * 2**20, transcendentals=0
        ),
    )(
        upstream.reshape(total, -1),
        centers,
        post_relu.reshape(total, -1),
        target_feats,
        out_weight,
    )


def shift(value, step, size):
    return lax.rem(value + step, size)


def tail_kernel(
    devices, teams, count,
    prod_ref, part_ref, relu_ref, input_ref, weight_ref, conv_ref,
    tgt_ref, act_ref, out_ref, taps_ref,
    got_core, got_pair, got_far, got_src, sum_core, sum_pair,
    edge, got_edge, padded, window, terms, got_half, held, got_rest, full,
    core_send, core_recv, pair_send, pair_recv, far_send, far_recv, src_send, src_recv,
    edge_send, edge_recv, half_send, half_recv, rest_send, rest_recv,
    all_send, all_recv, last_send, last_recv,
):
    s = lax.axis_index("src")
    t = lax.axis_index("tgt")
    groups = devices // 4
    size = devices * teams // 2
    tile, width, channels = input_ref.shape
    lines = terms.shape[0] // (2 * size)
    core, pair, far = lax.rem(s, 2), lax.rem(s // 2, 2), s // 4
    me = (s // 2) * teams + t
    spot = s * teams + t
    core_mate = (s + 1 - 2 * core, t)
    pair_mate = (s + 2 - 4 * pair, t)

    def far_mate(d):
        return (shift(far, d, groups) * 4 + pair * 2 + core, t)

    def place(rank):
        return (rank // teams * 2 + core, lax.rem(rank, teams))

    everyone = devices * teams
    up, down = shift(spot, everyone - 1, everyone), shift(spot, 1, everyone)
    above = (up // teams, lax.rem(up, teams))
    below = (down // teams, lax.rem(down, teams))
    has_above = spot > 0
    has_below = spot < devices * teams - 1

    barrier = pltpu.get_barrier_semaphore()
    pl.semaphore_signal(barrier, inc=1, device_id=core_mate, device_id_type=MESH)

    @pl.loop(1, size)
    def _(d):
        pl.semaphore_signal(
            barrier, inc=1, device_id=place(shift(me, d, size)), device_id_type=MESH
        )

    for device in (above, below):
        pl.semaphore_signal(barrier, inc=1, device_id=device, device_id_type=MESH)
    pl.semaphore_wait(barrier, size + 2)

    def remote(src, dst, send_sem, recv_sem, device):
        return pltpu.make_async_remote_copy(
            src_ref=src, dst_ref=dst, send_sem=send_sem, recv_sem=recv_sem,
            device_id=device, device_id_type=MESH,
        )

    def send(*args):
        copy = remote(*args)
        copy.start()
        return copy

    core_copies = [
        send(part_ref.at[q, 1 - core], got_core.at[q], core_send.at[q], core_recv.at[q], core_mate)
        for q in range(PIECES)
    ]
    src_copies = [
        send(
            prod_ref.at[shift(t, d, teams)], got_src.at[d - 1],
            src_send.at[d - 1], src_recv.at[d - 1], (s, shift(t, d, teams)),
        )
        for d in range(1, teams)
    ]
    pair_copies = []
    for q in range(PIECES):
        core_copies[q].wait()
        for half in range(2):
            value = part_ref[q, core, half].astype(jnp.float32)
            value = value + got_core[q, half].astype(jnp.float32)
            sum_core[q, half] = value.astype(jnp.bfloat16)
        pair_copies.append(
            send(sum_core.at[q, 1 - pair], got_pair.at[q], pair_send.at[q], pair_recv.at[q], pair_mate)
        )
    far_copies = []

    def far_step(q):
        pair_copies[q].wait()
        value = sum_core[q, pair].astype(jnp.float32) + got_pair[q].astype(jnp.float32)
        sum_pair[q] = value.astype(jnp.bfloat16)
        far_copies.append([
            send(
                sum_pair.at[q, shift(far, d, groups)], got_far.at[q, d - 1],
                far_send.at[q, d - 1], far_recv.at[q, d - 1], far_mate(d),
            )
            for d in range(1, groups)
        ])

    far_step(0)
    value = prod_ref[t].astype(jnp.float32)
    for d in range(1, teams):
        src_copies[d - 1].wait()
        value = value + got_src[d - 1].astype(jnp.float32)
    src_grad = value.astype(jnp.bfloat16)
    relu = relu_ref[pl.ds(t * tile, tile)].reshape(tile * width, channels)
    hidden = dot(src_grad, weight_ref[...], ((1,), (1,)))
    hidden = jnp.where(relu.astype(jnp.float32) > 0, hidden, 0.0)
    rounded = hidden.astype(jnp.bfloat16)
    edge[0] = rounded[:width]
    edge[1] = rounded[(tile - 1) * width :]

    def up_copy():
        return remote(edge.at[0], got_edge.at[1], edge_send.at[0], edge_recv.at[1], above)

    def down_copy():
        return remote(edge.at[1], got_edge.at[0], edge_send.at[1], edge_recv.at[0], below)

    @pl.when(has_above)
    def _():
        up_copy().start()

    @pl.when(has_below)
    def _():
        down_copy().start()

    padded[width : (tile + 1) * width] = rounded.astype(jnp.float32)
    out_term = dot(relu, src_grad, ((0,), (0,))).astype(jnp.bfloat16)
    for half in range(2):
        terms[half * channels : (half + 1) * channels] = out_term[:, half * 128 : (half + 1) * 128]
    for q in range(1, PIECES):
        far_step(q)

    @pl.when(has_above)
    def _():
        up_copy().wait_send()
        remote(edge.at[1], got_edge.at[0], edge_send.at[1], edge_recv.at[0], above).wait_recv()
        padded[0:width] = got_edge[0].astype(jnp.float32)

    @pl.when(jnp.logical_not(has_above))
    def _():
        padded[0:width] = jnp.zeros((width, channels), jnp.float32)

    @pl.when(has_below)
    def _():
        down_copy().wait_send()
        remote(edge.at[0], got_edge.at[1], edge_send.at[0], edge_recv.at[1], below).wait_recv()
        padded[(tile + 1) * width :] = got_edge[1].astype(jnp.float32)

    @pl.when(jnp.logical_not(has_below))
    def _():
        padded[(tile + 1) * width :] = jnp.zeros((width, channels), jnp.float32)

    whole = padded[...]
    total = whole.shape[0]
    column = lax.rem(lax.broadcasted_iota(jnp.int32, whole.shape, 0), width)
    right = jnp.where(column < width - 1, pltpu.roll(whole, total - 1, 0), 0.0)
    left = jnp.where(column > 0, pltpu.roll(whole, 1, 0), 0.0)
    for q, value in enumerate((right, whole, left)):
        window[:, q * channels : (q + 1) * channels] = value.astype(jnp.bfloat16)
    inputs = input_ref[...].reshape(tile * width, channels)
    base = 2 * channels
    for p in range(3):
        rows = window[(2 - p) * width : (2 - p + tile) * width]
        grads = dot(inputs, rows, ((0,), (0,))).astype(jnp.bfloat16)
        for q in range(3):
            first = base + (3 * p + q) * channels
            terms[first : first + channels] = grads[:, q * channels : (q + 1) * channels]
    used = base + 9 * channels
    if used < terms.shape[0]:
        terms[used:] = jnp.zeros((terms.shape[0] - used, 128), jnp.bfloat16)

    def rows_of(half, first, number):
        start = (half * size + first) * lines
        return pl.ds(pl.multiple_of(start, 16), number * lines)

    half_copy = send(terms.at[rows_of(1 - core, 0, size)], got_half, half_send, half_recv, core_mate)
    act = jnp.zeros((tile * width, channels), jnp.float32)
    for p in range(3):
        rows = window[(2 - p) * width : (2 - p + tile) * width]
        taps = jnp.concatenate([conv_ref[p, q] for q in range(3)], axis=1)
        act = act + dot(rows, taps, ((1,), (1,)))
    act_ref[...] = act.reshape(act_ref.shape).astype(act_ref.dtype)
    half_copy.wait()
    value = terms[rows_of(core, 0, size)].astype(jnp.float32) + got_half[...].astype(jnp.float32)
    held[...] = value.astype(jnp.bfloat16)

    def rest_copy(d):
        rank = shift(me, d, size)
        return remote(
            held.at[rows_of(0, rank, 1)], got_rest.at[d - 1],
            rest_send.at[d - 1], rest_recv.at[d - 1], place(rank),
        )

    @pl.loop(1, size)
    def _(d):
        rest_copy(d).start()

    depth = part_ref.shape[4]
    for q in range(PIECES):
        value = sum_pair[q, far].astype(jnp.float32)
        for d in range(1, groups):
            far_copies[q][d - 1].wait()
            value = value + got_far[q, d - 1].astype(jnp.float32)
        tgt_ref[q * depth : (q + 1) * depth] = value.astype(jnp.bfloat16)

    def add(d, value):
        rest_copy(d).wait()
        return value + got_rest[d - 1].astype(jnp.float32)

    value = lax.fori_loop(1, size, add, held[rows_of(0, me, 1)].astype(jnp.float32))
    full[rows_of(core, me, 1)] = value.astype(jnp.bfloat16)

    def all_copy(d, rank):
        rows = rows_of(core, rank, 1)
        return remote(
            full.at[rows], full.at[rows],
            all_send.at[d - 1], all_recv.at[d - 1], place(shift(me, d, size)),
        )

    @pl.loop(1, size)
    def _(d):
        all_copy(d, me).start()

    @pl.loop(1, size)
    def _(d):
        all_copy(d, me).wait_send()
        all_copy(d, shift(me, size - d, size)).wait_recv()

    mine = full.at[rows_of(core, 0, size)]
    other = full.at[rows_of(1 - core, 0, size)]
    remote(mine, mine, last_send, last_recv, core_mate).start()
    remote(mine, mine, last_send, last_recv, core_mate).wait_send()
    remote(other, other, last_send, last_recv, core_mate).wait_recv()
    for half in range(2):
        out_ref[:, half * 128 : (half + 1) * 128] = (
            full[half * channels : (half + 1) * channels].astype(jnp.float32) * (1.0 / count)
        )
    taps_ref[...] = full[base:used].astype(jnp.float32) * (1.0 / count)


def tail(product, part, post_relu, conv_input, out_weight, conv_weight, devices, teams):
    total, feat = product.shape
    share_rows = total // teams
    _, _, _, groups, lines, share, _ = part.shape
    tile, width, channels = conv_input.shape
    assert channels == 128 and feat == 256
    size = devices * teams // 2
    used = 11 * channels
    chunk = -(-used // (2 * size * 16)) * 16
    count = float(post_relu.shape[0] * devices)
    vmem = pl.BlockSpec(memory_space=pltpu.VMEM)
    block = (groups, lines, share, feat)
    dma = pltpu.SemaphoreType.DMA
    bf16 = jnp.bfloat16
    return pl.pallas_call(
        lambda *refs: tail_kernel(devices, teams, count, *refs),
        out_shape=(
            jax.ShapeDtypeStruct((PIECES * lines, share, feat), bf16),
            jax.ShapeDtypeStruct((tile, width, channels), bf16),
            jax.ShapeDtypeStruct((channels, feat), jnp.float32),
            jax.ShapeDtypeStruct((9 * channels, channels), jnp.float32),
        ),
        in_specs=[vmem] * 6,
        out_specs=(vmem,) * 4,
        scratch_shapes=[
            pltpu.VMEM((PIECES, 2) + block, bf16),
            pltpu.VMEM((PIECES,) + block, bf16),
            pltpu.VMEM((PIECES,) + block, bf16),
            pltpu.VMEM((teams, share_rows, feat), bf16),
            pltpu.VMEM((PIECES, 2) + block, bf16),
            pltpu.VMEM((PIECES,) + block, bf16),
            pltpu.VMEM((2, width, channels), bf16),
            pltpu.VMEM((2, width, channels), bf16),
            pltpu.VMEM(((tile + 2) * width, channels), jnp.float32),
            pltpu.VMEM(((tile + 2) * width, 3 * channels), bf16),
            pltpu.VMEM((2 * size * chunk, 128), bf16),
            pltpu.VMEM((size * chunk, 128), bf16),
            pltpu.VMEM((size * chunk, 128), bf16),
            pltpu.VMEM((size, chunk, 128), bf16),
            pltpu.VMEM((2 * size * chunk, 128), bf16),
            dma((PIECES,)), dma((PIECES,)), dma((PIECES,)), dma((PIECES,)),
            dma((PIECES, groups)), dma((PIECES, groups)),
            dma((teams,)), dma((teams,)),
            dma((2,)), dma((2,)), dma, dma, dma((size,)), dma((size,)),
            dma((size,)), dma((size,)), dma, dma,
        ],
        compiler_params=pltpu.CompilerParams(
            collective_id=0, has_side_effects=True, vmem_limit_bytes=40 * 2**20
        ),
    )(
        product.reshape(teams, share_rows, feat), part, post_relu, conv_input, out_weight, conv_weight
    )


def body(upstream, centers, post_relu, conv_input, target_feats, out_weight, conv_weight):
    devices = lax.axis_size("src")
    teams = lax.axis_size("tgt")
    product, part = corr_grads(upstream, centers, post_relu, target_feats, out_weight, devices)
    tgt_grad, act_grad, out_wgrad, taps = tail(
        product, part, post_relu, conv_input, out_weight, conv_weight, devices, teams
    )
    return (tgt_grad, act_grad, out_wgrad, taps.reshape(conv_weight.shape))


def solution(mesh):
    placed = (
        P("src", None, None),
        P(None, "src", None),
        P("src", None, None),
        P(("src", "tgt"), None, None),
        P("tgt", None, None),
        P(),
        P(),
    )
    return jax.shard_map(
        body,
        mesh=mesh,
        in_specs=placed,
        out_specs=(P("tgt", "src", None), P(("src", "tgt"), None, None), P(), P()),
        check_vma=False,
    )
```

```python
import math

import jax
import jax.numpy as jnp
from jax import lax
from jax.experimental import pallas as pl
from jax.experimental.pallas import tpu as pltpu
from jax.sharding import PartitionSpec as P

OFFSET = (0, 81, 34, 115)
EMPTY = (100, 178, 120, 208)
FAR = 4096
PIECES = 2
MESH = pl.DeviceIdType.MESH


def dot(a, b, dims=((1,), (0,))):
    return lax.dot_general(a, b, (dims, ((), ())), preferred_element_type=jnp.float32)


def spread_matrix(half, width, transposed):
    shape = (384, width) if transposed else (width, 384)
    cell = lax.broadcasted_iota(jnp.int32, shape, 0 if transposed else 1)
    col = lax.broadcasted_iota(jnp.int32, shape, 1 if transposed else 0)
    one = jnp.where(cell == (col >> 1), 0.25, 0.0)
    two = jnp.where(cell == 128 + 64 * half + (col >> 2), 0.0625, 0.0)
    three = jnp.where(cell == 256 + (col >> 3), 0.015625, 0.0)
    return (one + two + three).astype(jnp.bfloat16)


def build_table(row_first, up_ref, cen_ref, rows_ref, cols_ref, tail_ref, table_ref):
    total = up_ref.shape[0]
    for r in range(total // 128):
        for part, ref in ((0, rows_ref), (1, cols_ref)):
            line = jnp.broadcast_to(cen_ref[part, r : r + 1, :], (128, 128))
            ref[r * 128 : (r + 1) * 128, :] = jnp.transpose(line)
    tail_ref[:, 0:68] = up_ref[:, 256:324].astype(jnp.float32)
    lane = lax.broadcasted_iota(jnp.int32, (16, 128), 1)

    @pl.loop(0, total // 16, unroll=2)
    def _(group):
        here = pl.ds(pl.multiple_of(group * 16, 16), 16)
        first = up_ref[here, 0:128].astype(jnp.float32)
        second = up_ref[here, 128:256].astype(jnp.float32)
        third = tail_ref[here, :]
        source = (
            jnp.where(lane < 81, first, 0.0),
            jnp.where(lane >= 81, first, jnp.where(lane < 34, second, 0.0)),
            jnp.where((lane >= 34) & (lane < 115), second, 0.0),
            jnp.where(lane >= 115, second, jnp.where(lane < 68, third, 0.0)),
        )
        center_row = rows_ref[here, :]
        center_col = cols_ref[here, :]

        def row_term(level, cell):
            a = cell + ((row_first >> level) + 4) - (center_row >> level)
            return jnp.where((a >= 0) & (a < 9), 9 * a + OFFSET[level], FAR)

        def col_term(level, cell):
            b = cell + 4 - (center_col >> level)
            return jnp.where((b >= 0) & (b < 9), b, FAR)

        def put(level, tile, index):
            index = jnp.minimum(index, EMPTY[level]) & 127
            value = jnp.take_along_axis(source[level], index, axis=1, mode="promise_in_bounds")
            table_ref[here, tile * 128 : (tile + 1) * 128] = value.astype(jnp.bfloat16)

        halves = [col_term(0, lane + 128 * h) for h in range(2)]
        for y in range(8):
            a = row_term(0, y)
            for h in range(2):
                put(0, 2 * y + h, a + halves[h])
        b = col_term(1, lane)
        for j in range(4):
            put(1, 16 + j, row_term(1, j) + b)
        put(2, 20, row_term(2, lane >> 6) + col_term(2, lane & 63))
        put(3, 21, jnp.where(lane < 32, row_term(3, 0) + col_term(3, lane), FAR))


def corr_kernel(
    up_ref, cen_ref, relu_ref, tf_ref, ow_ref,
    src_ref, tgt_ref,
    rows_ref, cols_ref, tail_ref, table_ref, pooled_ref, sums_ref, feats_ref,
):
    total = up_ref.shape[0]
    width = tf_ref.shape[1]
    feat = tf_ref.shape[2]
    dense = tf_ref.shape[0] * width
    scale = 1.0 / math.sqrt(feat)
    row_first = lax.axis_index("tgt") * tf_ref.shape[0]
    build_table(row_first, up_ref, cen_ref, rows_ref, cols_ref, tail_ref, table_ref)

    mats = [spread_matrix(half, width, True) for half in range(2)]
    coarse = jnp.zeros((256, feat), jnp.float32)
    for j in range(4):
        fine = jnp.zeros((128, feat), jnp.float32)
        for y in (2 * j, 2 * j + 1):
            part = dot(mats[y // 4], tf_ref[y])
            fine = fine + part[:128]
            coarse = coarse + part[128:]
        pooled_ref[j * 128 : (j + 1) * 128, :] = fine.astype(jnp.bfloat16)
    pooled_ref[512:768, :] = coarse.astype(jnp.bfloat16)

    feats_ref[...] = dot(ow_ref[...], relu_ref[...], ((0,), (1,))).astype(jnp.bfloat16)

    @pl.loop(0, total // 256)
    def _(block):
        here = pl.ds(pl.multiple_of(block * 256, 256), 256)
        value = dot(table_ref[here, :dense], tf_ref[...].reshape(dense, feat))
        value = value + dot(table_ref[here, dense:], pooled_ref[...])
        src_ref[here, :] = (value * scale).astype(src_ref.dtype)

    @pl.loop(0, table_ref.shape[1] // 256)
    def _(tile):
        here = pl.ds(pl.multiple_of(tile * 256, 256), 256)
        sums_ref[:, here] = dot(feats_ref[...], table_ref[:, here]).astype(jnp.bfloat16)

    eye = (
        lax.broadcasted_iota(jnp.int32, (width, width), 0)
        == lax.broadcasted_iota(jnp.int32, (width, width), 1)
    )
    eye = jnp.where(eye, 1.0, 0.0).astype(jnp.bfloat16)
    for y in range(8):
        mat = spread_matrix(y // 4, width, False)
        j = y // 2
        value = dot(eye, sums_ref[:, y * 256 : (y + 1) * 256], ((1,), (1,)))
        value = value + dot(
            mat[:, :128], sums_ref[:, dense + j * 128 : dense + (j + 1) * 128], ((1,), (1,))
        )
        value = value + dot(mat[:, 128:], sums_ref[:, dense + 512 :], ((1,), (1,)))
        value = (value * scale).astype(tgt_ref.dtype)
        pieces, _, _, groups, lines, share, _ = tgt_ref.shape
        for k in range(4 * groups):
            tgt_ref[y // lines, k % 2, k // 2 % 2, k // 4, y % lines] = value[
                k * share : (k + 1) * share
            ]


def corr_grads(upstream, centers, post_relu, target_feats, out_weight, devices):
    total = upstream.shape[0] * upstream.shape[1]
    rows, width, feat = target_feats.shape
    assert rows == 8 and width == 256
    cells = rows * width + 768
    vmem = pl.BlockSpec(memory_space=pltpu.VMEM)
    return pl.pallas_call(
        corr_kernel,
        out_shape=(
            jax.ShapeDtypeStruct((total, feat), jnp.bfloat16),
            jax.ShapeDtypeStruct(
                (PIECES, 2, 2, devices // 4, rows // PIECES, width // devices, feat), jnp.bfloat16
            ),
        ),
        in_specs=[vmem] * 5,
        out_specs=(vmem, vmem),
        scratch_shapes=[
            pltpu.VMEM((total, 128), jnp.int32),
            pltpu.VMEM((total, 128), jnp.int32),
            pltpu.VMEM((total, 128), jnp.float32),
            pltpu.VMEM((total, cells), jnp.bfloat16),
            pltpu.VMEM((768, feat), jnp.bfloat16),
            pltpu.VMEM((feat, cells), jnp.bfloat16),
            pltpu.VMEM((feat, total), jnp.bfloat16),
        ],
        compiler_params=pltpu.CompilerParams(vmem_limit_bytes=48 * 2**20),
        cost_estimate=pl.CostEstimate(
            flops=4 * total * cells * feat, bytes_accessed=6 * 2**20, transcendentals=0
        ),
    )(
        upstream.reshape(total, -1),
        centers,
        post_relu.reshape(total, -1),
        target_feats,
        out_weight,
    )


def shift(value, step, size):
    return lax.rem(value + step, size)


def tail_kernel(
    devices, teams, count,
    prod_ref, part_ref, relu_ref, input_ref, weight_ref, conv_ref,
    tgt_ref, act_ref, out_ref, taps_ref,
    got_core, got_pair, got_far, got_src, sum_core, sum_pair,
    edge, got_edge, padded, window, terms, got_half, held, got_rest, full,
    core_send, core_recv, pair_send, pair_recv, far_send, far_recv, src_send, src_recv,
    edge_send, edge_recv, half_send, half_recv, rest_send, rest_recv,
    all_send, all_recv, last_send, last_recv,
):
    s = lax.axis_index("src")
    t = lax.axis_index("tgt")
    groups = devices // 4
    size = devices * teams // 2
    tile, width, channels = input_ref.shape
    lines = terms.shape[0] // (2 * size)
    core, pair, far = lax.rem(s, 2), lax.rem(s // 2, 2), s // 4
    me = (s // 2) * teams + t
    spot = s * teams + t
    core_mate = (s + 1 - 2 * core, t)
    pair_mate = (s + 2 - 4 * pair, t)

    def far_mate(d):
        return (shift(far, d, groups) * 4 + pair * 2 + core, t)

    def place(rank):
        return (rank // teams * 2 + core, lax.rem(rank, teams))

    everyone = devices * teams
    up, down = shift(spot, everyone - 1, everyone), shift(spot, 1, everyone)
    above = (up // teams, lax.rem(up, teams))
    below = (down // teams, lax.rem(down, teams))
    has_above = spot > 0
    has_below = spot < devices * teams - 1

    barrier = pltpu.get_barrier_semaphore()
    pl.semaphore_signal(barrier, inc=1, device_id=core_mate, device_id_type=MESH)

    @pl.loop(1, size)
    def _(d):
        pl.semaphore_signal(
            barrier, inc=1, device_id=place(shift(me, d, size)), device_id_type=MESH
        )

    for device in (above, below):
        pl.semaphore_signal(barrier, inc=1, device_id=device, device_id_type=MESH)
    pl.semaphore_wait(barrier, size + 2)

    def remote(src, dst, send_sem, recv_sem, device):
        return pltpu.make_async_remote_copy(
            src_ref=src, dst_ref=dst, send_sem=send_sem, recv_sem=recv_sem,
            device_id=device, device_id_type=MESH,
        )

    def send(*args):
        copy = remote(*args)
        copy.start()
        return copy

    core_copies = [
        send(part_ref.at[q, 1 - core], got_core.at[q], core_send.at[q], core_recv.at[q], core_mate)
        for q in range(PIECES)
    ]
    src_copies = [
        send(
            prod_ref.at[shift(t, d, teams)], got_src.at[d - 1],
            src_send.at[d - 1], src_recv.at[d - 1], (s, shift(t, d, teams)),
        )
        for d in range(1, teams)
    ]
    pair_copies = []
    for q in range(PIECES):
        core_copies[q].wait()
        for half in range(2):
            value = part_ref[q, core, half].astype(jnp.float32)
            value = value + got_core[q, half].astype(jnp.float32)
            sum_core[q, half] = value.astype(jnp.bfloat16)
        pair_copies.append(
            send(sum_core.at[q, 1 - pair], got_pair.at[q], pair_send.at[q], pair_recv.at[q], pair_mate)
        )
    far_copies = []

    def far_step(q):
        pair_copies[q].wait()
        value = sum_core[q, pair].astype(jnp.float32) + got_pair[q].astype(jnp.float32)
        sum_pair[q] = value.astype(jnp.bfloat16)
        far_copies.append([
            send(
                sum_pair.at[q, shift(far, d, groups)], got_far.at[q, d - 1],
                far_send.at[q, d - 1], far_recv.at[q, d - 1], far_mate(d),
            )
            for d in range(1, groups)
        ])

    far_step(0)
    value = prod_ref[t].astype(jnp.float32)
    for d in range(1, teams):
        src_copies[d - 1].wait()
        value = value + got_src[d - 1].astype(jnp.float32)
    src_grad = value.astype(jnp.bfloat16)
    relu = relu_ref[pl.ds(t * tile, tile)].reshape(tile * width, channels)
    hidden = dot(src_grad, weight_ref[...], ((1,), (1,)))
    hidden = jnp.where(relu.astype(jnp.float32) > 0, hidden, 0.0)
    rounded = hidden.astype(jnp.bfloat16)
    edge[0] = rounded[:width]
    edge[1] = rounded[(tile - 1) * width :]

    def up_copy():
        return remote(edge.at[0], got_edge.at[1], edge_send.at[0], edge_recv.at[1], above)

    def down_copy():
        return remote(edge.at[1], got_edge.at[0], edge_send.at[1], edge_recv.at[0], below)

    @pl.when(has_above)
    def _():
        up_copy().start()

    @pl.when(has_below)
    def _():
        down_copy().start()

    padded[width : (tile + 1) * width] = rounded.astype(jnp.float32)
    out_term = dot(relu, src_grad, ((0,), (0,))).astype(jnp.bfloat16)
    for half in range(2):
        terms[half * channels : (half + 1) * channels] = out_term[:, half * 128 : (half + 1) * 128]
    for q in range(1, PIECES):
        far_step(q)

    @pl.when(has_above)
    def _():
        up_copy().wait_send()
        remote(edge.at[1], got_edge.at[0], edge_send.at[1], edge_recv.at[0], above).wait_recv()
        padded[0:width] = got_edge[0].astype(jnp.float32)

    @pl.when(jnp.logical_not(has_above))
    def _():
        padded[0:width] = jnp.zeros((width, channels), jnp.float32)

    @pl.when(has_below)
    def _():
        down_copy().wait_send()
        remote(edge.at[0], got_edge.at[1], edge_send.at[0], edge_recv.at[1], below).wait_recv()
        padded[(tile + 1) * width :] = got_edge[1].astype(jnp.float32)

    @pl.when(jnp.logical_not(has_below))
    def _():
        padded[(tile + 1) * width :] = jnp.zeros((width, channels), jnp.float32)

    whole = padded[...]
    total = whole.shape[0]
    column = lax.rem(lax.broadcasted_iota(jnp.int32, whole.shape, 0), width)
    right = jnp.where(column < width - 1, pltpu.roll(whole, total - 1, 0), 0.0)
    left = jnp.where(column > 0, pltpu.roll(whole, 1, 0), 0.0)
    for q, value in enumerate((right, whole, left)):
        window[:, q * channels : (q + 1) * channels] = value.astype(jnp.bfloat16)
    inputs = input_ref[...].reshape(tile * width, channels)
    base = 2 * channels
    for p in range(3):
        rows = window[(2 - p) * width : (2 - p + tile) * width]
        grads = dot(inputs, rows, ((0,), (0,))).astype(jnp.bfloat16)
        for q in range(3):
            first = base + (3 * p + q) * channels
            terms[first : first + channels] = grads[:, q * channels : (q + 1) * channels]
    used = base + 9 * channels
    if used < terms.shape[0]:
        terms[used:] = jnp.zeros((terms.shape[0] - used, 128), jnp.bfloat16)

    def rows_of(half, first, number):
        start = (half * size + first) * lines
        return pl.ds(pl.multiple_of(start, 16), number * lines)

    half_copy = send(terms.at[rows_of(1 - core, 0, size)], got_half, half_send, half_recv, core_mate)
    act = jnp.zeros((tile * width, channels), jnp.float32)
    for p in range(3):
        rows = window[(2 - p) * width : (2 - p + tile) * width]
        taps = jnp.concatenate([conv_ref[p, q] for q in range(3)], axis=1)
        act = act + dot(rows, taps, ((1,), (1,)))
    act_ref[...] = act.reshape(act_ref.shape).astype(act_ref.dtype)
    half_copy.wait()
    value = terms[rows_of(core, 0, size)].astype(jnp.float32) + got_half[...].astype(jnp.float32)
    held[...] = value.astype(jnp.bfloat16)

    def rest_copy(d):
        rank = shift(me, d, size)
        return remote(
            held.at[rows_of(0, rank, 1)], got_rest.at[d - 1],
            rest_send.at[d - 1], rest_recv.at[d - 1], place(rank),
        )

    @pl.loop(1, size)
    def _(d):
        rest_copy(d).start()

    def add(d, value):
        rest_copy(d).wait()
        return value + got_rest[d - 1].astype(jnp.float32)

    value = lax.fori_loop(1, size, add, held[rows_of(0, me, 1)].astype(jnp.float32))
    full[rows_of(core, me, 1)] = value.astype(jnp.bfloat16)

    def all_copy(d, rank):
        rows = rows_of(core, rank, 1)
        return remote(
            full.at[rows], full.at[rows],
            all_send.at[d - 1], all_recv.at[d - 1], place(shift(me, d, size)),
        )

    @pl.loop(1, size)
    def _(d):
        all_copy(d, me).start()

    depth = part_ref.shape[4]
    for q in range(PIECES):
        value = sum_pair[q, far].astype(jnp.float32)
        for d in range(1, groups):
            far_copies[q][d - 1].wait()
            value = value + got_far[q, d - 1].astype(jnp.float32)
        tgt_ref[q * depth : (q + 1) * depth] = value.astype(jnp.bfloat16)

    @pl.loop(1, size)
    def _(d):
        all_copy(d, me).wait_send()
        all_copy(d, shift(me, size - d, size)).wait_recv()

    mine = full.at[rows_of(core, 0, size)]
    other = full.at[rows_of(1 - core, 0, size)]
    remote(mine, mine, last_send, last_recv, core_mate).start()
    remote(mine, mine, last_send, last_recv, core_mate).wait_send()
    remote(other, other, last_send, last_recv, core_mate).wait_recv()
    for half in range(2):
        out_ref[:, half * 128 : (half + 1) * 128] = (
            full[half * channels : (half + 1) * channels].astype(jnp.float32) * (1.0 / count)
        )
    taps_ref[...] = full[base:used].astype(jnp.float32) * (1.0 / count)


def tail(product, part, post_relu, conv_input, out_weight, conv_weight, devices, teams):
    total, feat = product.shape
    share_rows = total // teams
    _, _, _, groups, lines, share, _ = part.shape
    tile, width, channels = conv_input.shape
    assert channels == 128 and feat == 256
    size = devices * teams // 2
    used = 11 * channels
    chunk = -(-used // (2 * size * 16)) * 16
    count = float(post_relu.shape[0] * devices)
    vmem = pl.BlockSpec(memory_space=pltpu.VMEM)
    block = (groups, lines, share, feat)
    dma = pltpu.SemaphoreType.DMA
    bf16 = jnp.bfloat16
    return pl.pallas_call(
        lambda *refs: tail_kernel(devices, teams, count, *refs),
        out_shape=(
            jax.ShapeDtypeStruct((PIECES * lines, share, feat), bf16),
            jax.ShapeDtypeStruct((tile, width, channels), bf16),
            jax.ShapeDtypeStruct((channels, feat), jnp.float32),
            jax.ShapeDtypeStruct((9 * channels, channels), jnp.float32),
        ),
        in_specs=[vmem] * 6,
        out_specs=(vmem,) * 4,
        scratch_shapes=[
            pltpu.VMEM((PIECES, 2) + block, bf16),
            pltpu.VMEM((PIECES,) + block, bf16),
            pltpu.VMEM((PIECES,) + block, bf16),
            pltpu.VMEM((teams, share_rows, feat), bf16),
            pltpu.VMEM((PIECES, 2) + block, bf16),
            pltpu.VMEM((PIECES,) + block, bf16),
            pltpu.VMEM((2, width, channels), bf16),
            pltpu.VMEM((2, width, channels), bf16),
            pltpu.VMEM(((tile + 2) * width, channels), jnp.float32),
            pltpu.VMEM(((tile + 2) * width, 3 * channels), bf16),
            pltpu.VMEM((2 * size * chunk, 128), bf16),
            pltpu.VMEM((size * chunk, 128), bf16),
            pltpu.VMEM((size * chunk, 128), bf16),
            pltpu.VMEM((size, chunk, 128), bf16),
            pltpu.VMEM((2 * size * chunk, 128), bf16),
            dma((PIECES,)), dma((PIECES,)), dma((PIECES,)), dma((PIECES,)),
            dma((PIECES, groups)), dma((PIECES, groups)),
            dma((teams,)), dma((teams,)),
            dma((2,)), dma((2,)), dma, dma, dma((size,)), dma((size,)),
            dma((size,)), dma((size,)), dma, dma,
        ],
        compiler_params=pltpu.CompilerParams(
            collective_id=0, has_side_effects=True, vmem_limit_bytes=40 * 2**20
        ),
    )(
        product.reshape(teams, share_rows, feat), part, post_relu, conv_input, out_weight, conv_weight
    )


def body(upstream, centers, post_relu, conv_input, target_feats, out_weight, conv_weight):
    devices = lax.axis_size("src")
    teams = lax.axis_size("tgt")
    product, part = corr_grads(upstream, centers, post_relu, target_feats, out_weight, devices)
    tgt_grad, act_grad, out_wgrad, taps = tail(
        product, part, post_relu, conv_input, out_weight, conv_weight, devices, teams
    )
    return (tgt_grad, act_grad, out_wgrad, taps.reshape(conv_weight.shape))


def solution(mesh):
    placed = (
        P("src", None, None),
        P(None, "src", None),
        P("src", None, None),
        P(("src", "tgt"), None, None),
        P("tgt", None, None),
        P(),
        P(),
    )
    return jax.shard_map(
        body,
        mesh=mesh,
        in_specs=placed,
        out_specs=(P("tgt", "src", None), P(("src", "tgt"), None, None), P(), P()),
        check_vma=False,
    )
```

```python
import math

import jax
import jax.numpy as jnp
from jax import lax
from jax.experimental import pallas as pl
from jax.experimental.pallas import tpu as pltpu
from jax.sharding import PartitionSpec as P

OFFSET = (0, 81, 34, 115)
EMPTY = (100, 178, 120, 208)
FAR = 4096
PIECES = 2
MESH = pl.DeviceIdType.MESH


def dot(a, b, dims=((1,), (0,))):
    return lax.dot_general(a, b, (dims, ((), ())), preferred_element_type=jnp.float32)


def spread_matrix(half, width, transposed):
    shape = (384, width) if transposed else (width, 384)
    cell = lax.broadcasted_iota(jnp.int32, shape, 0 if transposed else 1)
    col = lax.broadcasted_iota(jnp.int32, shape, 1 if transposed else 0)
    one = jnp.where(cell == (col >> 1), 0.25, 0.0)
    two = jnp.where(cell == 128 + 64 * half + (col >> 2), 0.0625, 0.0)
    three = jnp.where(cell == 256 + (col >> 3), 0.015625, 0.0)
    return (one + two + three).astype(jnp.bfloat16)


def build_table(row_first, up_ref, cen_ref, rows_ref, cols_ref, tail_ref, table_ref):
    total = up_ref.shape[0]
    for r in range(total // 128):
        for part, ref in ((0, rows_ref), (1, cols_ref)):
            line = jnp.broadcast_to(cen_ref[part, r : r + 1, :], (128, 128))
            ref[r * 128 : (r + 1) * 128, :] = jnp.transpose(line)
    tail_ref[:, 0:68] = up_ref[:, 256:324].astype(jnp.float32)
    lane = lax.broadcasted_iota(jnp.int32, (16, 128), 1)

    @pl.loop(0, total // 16, unroll=4)
    def _(group):
        here = pl.ds(pl.multiple_of(group * 16, 16), 16)
        first = up_ref[here, 0:128].astype(jnp.float32)
        second = up_ref[here, 128:256].astype(jnp.float32)
        third = tail_ref[here, :]
        source = (
            jnp.where(lane < 81, first, 0.0),
            jnp.where(lane >= 81, first, jnp.where(lane < 34, second, 0.0)),
            jnp.where((lane >= 34) & (lane < 115), second, 0.0),
            jnp.where(lane >= 115, second, jnp.where(lane < 68, third, 0.0)),
        )
        center_row = rows_ref[here, :]
        center_col = cols_ref[here, :]

        def row_term(level, cell):
            a = cell + ((row_first >> level) + 4) - (center_row >> level)
            return jnp.where((a >= 0) & (a < 9), 9 * a + OFFSET[level], FAR)

        def col_term(level, cell):
            b = cell + 4 - (center_col >> level)
            return jnp.where((b >= 0) & (b < 9), b, FAR)

        def put(level, tile, index):
            index = jnp.minimum(index, EMPTY[level]) & 127
            value = jnp.take_along_axis(source[level], index, axis=1, mode="promise_in_bounds")
            table_ref[here, tile * 128 : (tile + 1) * 128] = value.astype(jnp.bfloat16)

        halves = [col_term(0, lane + 128 * h) for h in range(2)]
        for y in range(8):
            a = row_term(0, y)
            for h in range(2):
                put(0, 2 * y + h, a + halves[h])
        b = col_term(1, lane)
        for j in range(4):
            put(1, 16 + j, row_term(1, j) + b)
        put(2, 20, row_term(2, lane >> 6) + col_term(2, lane & 63))
        put(3, 21, jnp.where(lane < 32, row_term(3, 0) + col_term(3, lane), FAR))


def corr_kernel(
    up_ref, cen_ref, relu_ref, tf_ref, ow_ref,
    src_ref, tgt_ref,
    rows_ref, cols_ref, tail_ref, table_ref, pooled_ref, sums_ref, feats_ref,
):
    total = up_ref.shape[0]
    width = tf_ref.shape[1]
    feat = tf_ref.shape[2]
    dense = tf_ref.shape[0] * width
    scale = 1.0 / math.sqrt(feat)
    row_first = lax.axis_index("tgt") * tf_ref.shape[0]
    build_table(row_first, up_ref, cen_ref, rows_ref, cols_ref, tail_ref, table_ref)

    mats = [spread_matrix(half, width, True) for half in range(2)]
    coarse = jnp.zeros((256, feat), jnp.float32)
    for j in range(4):
        fine = jnp.zeros((128, feat), jnp.float32)
        for y in (2 * j, 2 * j + 1):
            part = dot(mats[y // 4], tf_ref[y])
            fine = fine + part[:128]
            coarse = coarse + part[128:]
        pooled_ref[j * 128 : (j + 1) * 128, :] = fine.astype(jnp.bfloat16)
    pooled_ref[512:768, :] = coarse.astype(jnp.bfloat16)

    feats_ref[...] = dot(ow_ref[...], relu_ref[...], ((0,), (1,))).astype(jnp.bfloat16)

    @pl.loop(0, total // 256)
    def _(block):
        here = pl.ds(pl.multiple_of(block * 256, 256), 256)
        value = dot(table_ref[here, :dense], tf_ref[...].reshape(dense, feat))
        value = value + dot(table_ref[here, dense:], pooled_ref[...])
        src_ref[here, :] = (value * scale).astype(src_ref.dtype)

    @pl.loop(0, table_ref.shape[1] // 256)
    def _(tile):
        here = pl.ds(pl.multiple_of(tile * 256, 256), 256)
        sums_ref[:, here] = dot(feats_ref[...], table_ref[:, here]).astype(jnp.bfloat16)

    eye = (
        lax.broadcasted_iota(jnp.int32, (width, width), 0)
        == lax.broadcasted_iota(jnp.int32, (width, width), 1)
    )
    eye = jnp.where(eye, 1.0, 0.0).astype(jnp.bfloat16)
    for y in range(8):
        mat = spread_matrix(y // 4, width, False)
        j = y // 2
        value = dot(eye, sums_ref[:, y * 256 : (y + 1) * 256], ((1,), (1,)))
        value = value + dot(
            mat[:, :128], sums_ref[:, dense + j * 128 : dense + (j + 1) * 128], ((1,), (1,))
        )
        value = value + dot(mat[:, 128:], sums_ref[:, dense + 512 :], ((1,), (1,)))
        value = (value * scale).astype(tgt_ref.dtype)
        pieces, _, _, groups, lines, share, _ = tgt_ref.shape
        for k in range(4 * groups):
            tgt_ref[y // lines, k % 2, k // 2 % 2, k // 4, y % lines] = value[
                k * share : (k + 1) * share
            ]


def corr_grads(upstream, centers, post_relu, target_feats, out_weight, devices):
    total = upstream.shape[0] * upstream.shape[1]
    rows, width, feat = target_feats.shape
    assert rows == 8 and width == 256
    cells = rows * width + 768
    vmem = pl.BlockSpec(memory_space=pltpu.VMEM)
    return pl.pallas_call(
        corr_kernel,
        out_shape=(
            jax.ShapeDtypeStruct((total, feat), jnp.bfloat16),
            jax.ShapeDtypeStruct(
                (PIECES, 2, 2, devices // 4, rows // PIECES, width // devices, feat), jnp.bfloat16
            ),
        ),
        in_specs=[vmem] * 5,
        out_specs=(vmem, vmem),
        scratch_shapes=[
            pltpu.VMEM((total, 128), jnp.int32),
            pltpu.VMEM((total, 128), jnp.int32),
            pltpu.VMEM((total, 128), jnp.float32),
            pltpu.VMEM((total, cells), jnp.bfloat16),
            pltpu.VMEM((768, feat), jnp.bfloat16),
            pltpu.VMEM((feat, cells), jnp.bfloat16),
            pltpu.VMEM((feat, total), jnp.bfloat16),
        ],
        compiler_params=pltpu.CompilerParams(vmem_limit_bytes=48 * 2**20),
        cost_estimate=pl.CostEstimate(
            flops=4 * total * cells * feat, bytes_accessed=6 * 2**20, transcendentals=0
        ),
    )(
        upstream.reshape(total, -1),
        centers,
        post_relu.reshape(total, -1),
        target_feats,
        out_weight,
    )


def shift(value, step, size):
    return lax.rem(value + step, size)


def tail_kernel(
    devices, teams, count,
    prod_ref, part_ref, relu_ref, input_ref, weight_ref, conv_ref,
    tgt_ref, act_ref, out_ref, taps_ref,
    got_core, got_pair, got_far, got_src, sum_core, sum_pair,
    edge, got_edge, padded, window, terms, got_half, held, got_rest, full,
    core_send, core_recv, pair_send, pair_recv, far_send, far_recv, src_send, src_recv,
    edge_send, edge_recv, half_send, half_recv, rest_send, rest_recv,
    all_send, all_recv, last_send, last_recv,
):
    s = lax.axis_index("src")
    t = lax.axis_index("tgt")
    groups = devices // 4
    size = devices * teams // 2
    tile, width, channels = input_ref.shape
    lines = terms.shape[0] // (2 * size)
    core, pair, far = lax.rem(s, 2), lax.rem(s // 2, 2), s // 4
    me = (s // 2) * teams + t
    spot = s * teams + t
    core_mate = (s + 1 - 2 * core, t)
    pair_mate = (s + 2 - 4 * pair, t)

    def far_mate(d):
        return (shift(far, d, groups) * 4 + pair * 2 + core, t)

    def place(rank):
        return (rank // teams * 2 + core, lax.rem(rank, teams))

    everyone = devices * teams
    up, down = shift(spot, everyone - 1, everyone), shift(spot, 1, everyone)
    above = (up // teams, lax.rem(up, teams))
    below = (down // teams, lax.rem(down, teams))
    has_above = spot > 0
    has_below = spot < devices * teams - 1

    barrier = pltpu.get_barrier_semaphore()
    pl.semaphore_signal(barrier, inc=1, device_id=core_mate, device_id_type=MESH)

    @pl.loop(1, size)
    def _(d):
        pl.semaphore_signal(
            barrier, inc=1, device_id=place(shift(me, d, size)), device_id_type=MESH
        )

    for device in (above, below):
        pl.semaphore_signal(barrier, inc=1, device_id=device, device_id_type=MESH)
    pl.semaphore_wait(barrier, size + 2)

    def remote(src, dst, send_sem, recv_sem, device):
        return pltpu.make_async_remote_copy(
            src_ref=src, dst_ref=dst, send_sem=send_sem, recv_sem=recv_sem,
            device_id=device, device_id_type=MESH,
        )

    def send(*args):
        copy = remote(*args)
        copy.start()
        return copy

    core_copies = [
        send(part_ref.at[q, 1 - core], got_core.at[q], core_send.at[q], core_recv.at[q], core_mate)
        for q in range(PIECES)
    ]
    src_copies = [
        send(
            prod_ref.at[shift(t, d, teams)], got_src.at[d - 1],
            src_send.at[d - 1], src_recv.at[d - 1], (s, shift(t, d, teams)),
        )
        for d in range(1, teams)
    ]
    pair_copies = []
    for q in range(PIECES):
        core_copies[q].wait()
        for half in range(2):
            value = part_ref[q, core, half].astype(jnp.float32)
            value = value + got_core[q, half].astype(jnp.float32)
            sum_core[q, half] = value.astype(jnp.bfloat16)
        pair_copies.append(
            send(sum_core.at[q, 1 - pair], got_pair.at[q], pair_send.at[q], pair_recv.at[q], pair_mate)
        )
    far_copies = []

    def far_step(q):
        pair_copies[q].wait()
        value = sum_core[q, pair].astype(jnp.float32) + got_pair[q].astype(jnp.float32)
        sum_pair[q] = value.astype(jnp.bfloat16)
        far_copies.append([
            send(
                sum_pair.at[q, shift(far, d, groups)], got_far.at[q, d - 1],
                far_send.at[q, d - 1], far_recv.at[q, d - 1], far_mate(d),
            )
            for d in range(1, groups)
        ])

    far_step(0)
    value = prod_ref[t].astype(jnp.float32)
    for d in range(1, teams):
        src_copies[d - 1].wait()
        value = value + got_src[d - 1].astype(jnp.float32)
    src_grad = value.astype(jnp.bfloat16)
    relu = relu_ref[pl.ds(t * tile, tile)].reshape(tile * width, channels)
    hidden = dot(src_grad, weight_ref[...], ((1,), (1,)))
    hidden = jnp.where(relu.astype(jnp.float32) > 0, hidden, 0.0)
    rounded = hidden.astype(jnp.bfloat16)
    edge[0] = rounded[:width]
    edge[1] = rounded[(tile - 1) * width :]

    def up_copy():
        return remote(edge.at[0], got_edge.at[1], edge_send.at[0], edge_recv.at[1], above)

    def down_copy():
        return remote(edge.at[1], got_edge.at[0], edge_send.at[1], edge_recv.at[0], below)

    @pl.when(has_above)
    def _():
        up_copy().start()

    @pl.when(has_below)
    def _():
        down_copy().start()

    padded[width : (tile + 1) * width] = rounded.astype(jnp.float32)
    out_term = dot(relu, src_grad, ((0,), (0,))).astype(jnp.bfloat16)
    for half in range(2):
        terms[half * channels : (half + 1) * channels] = out_term[:, half * 128 : (half + 1) * 128]
    for q in range(1, PIECES):
        far_step(q)

    @pl.when(has_above)
    def _():
        up_copy().wait_send()
        remote(edge.at[1], got_edge.at[0], edge_send.at[1], edge_recv.at[0], above).wait_recv()
        padded[0:width] = got_edge[0].astype(jnp.float32)

    @pl.when(jnp.logical_not(has_above))
    def _():
        padded[0:width] = jnp.zeros((width, channels), jnp.float32)

    @pl.when(has_below)
    def _():
        down_copy().wait_send()
        remote(edge.at[0], got_edge.at[1], edge_send.at[0], edge_recv.at[1], below).wait_recv()
        padded[(tile + 1) * width :] = got_edge[1].astype(jnp.float32)

    @pl.when(jnp.logical_not(has_below))
    def _():
        padded[(tile + 1) * width :] = jnp.zeros((width, channels), jnp.float32)

    whole = padded[...]
    total = whole.shape[0]
    column = lax.rem(lax.broadcasted_iota(jnp.int32, whole.shape, 0), width)
    right = jnp.where(column < width - 1, pltpu.roll(whole, total - 1, 0), 0.0)
    left = jnp.where(column > 0, pltpu.roll(whole, 1, 0), 0.0)
    for q, value in enumerate((right, whole, left)):
        window[:, q * channels : (q + 1) * channels] = value.astype(jnp.bfloat16)
    inputs = input_ref[...].reshape(tile * width, channels)
    base = 2 * channels
    for p in range(3):
        rows = window[(2 - p) * width : (2 - p + tile) * width]
        grads = dot(inputs, rows, ((0,), (0,))).astype(jnp.bfloat16)
        for q in range(3):
            first = base + (3 * p + q) * channels
            terms[first : first + channels] = grads[:, q * channels : (q + 1) * channels]
    used = base + 9 * channels
    if used < terms.shape[0]:
        terms[used:] = jnp.zeros((terms.shape[0] - used, 128), jnp.bfloat16)

    def rows_of(half, first, number):
        start = (half * size + first) * lines
        return pl.ds(pl.multiple_of(start, 16), number * lines)

    half_copy = send(terms.at[rows_of(1 - core, 0, size)], got_half, half_send, half_recv, core_mate)
    act = jnp.zeros((tile * width, channels), jnp.float32)
    for p in range(3):
        rows = window[(2 - p) * width : (2 - p + tile) * width]
        taps = jnp.concatenate([conv_ref[p, q] for q in range(3)], axis=1)
        act = act + dot(rows, taps, ((1,), (1,)))
    act_ref[...] = act.reshape(act_ref.shape).astype(act_ref.dtype)
    half_copy.wait()
    value = terms[rows_of(core, 0, size)].astype(jnp.float32) + got_half[...].astype(jnp.float32)
    held[...] = value.astype(jnp.bfloat16)

    def rest_copy(d):
        rank = shift(me, d, size)
        return remote(
            held.at[rows_of(0, rank, 1)], got_rest.at[d - 1],
            rest_send.at[d - 1], rest_recv.at[d - 1], place(rank),
        )

    @pl.loop(1, size)
    def _(d):
        rest_copy(d).start()

    def add(d, value):
        rest_copy(d).wait()
        return value + got_rest[d - 1].astype(jnp.float32)

    value = lax.fori_loop(1, size, add, held[rows_of(0, me, 1)].astype(jnp.float32))
    full[rows_of(core, me, 1)] = value.astype(jnp.bfloat16)

    def all_copy(d, rank):
        rows = rows_of(core, rank, 1)
        return remote(
            full.at[rows], full.at[rows],
            all_send.at[d - 1], all_recv.at[d - 1], place(shift(me, d, size)),
        )

    @pl.loop(1, size)
    def _(d):
        all_copy(d, me).start()

    depth = part_ref.shape[4]
    for q in range(PIECES):
        value = sum_pair[q, far].astype(jnp.float32)
        for d in range(1, groups):
            far_copies[q][d - 1].wait()
            value = value + got_far[q, d - 1].astype(jnp.float32)
        tgt_ref[q * depth : (q + 1) * depth] = value.astype(jnp.bfloat16)

    @pl.loop(1, size)
    def _(d):
        all_copy(d, me).wait_send()
        all_copy(d, shift(me, size - d, size)).wait_recv()

    mine = full.at[rows_of(core, 0, size)]
    other = full.at[rows_of(1 - core, 0, size)]
    remote(mine, mine, last_send, last_recv, core_mate).start()
    remote(mine, mine, last_send, last_recv, core_mate).wait_send()
    remote(other, other, last_send, last_recv, core_mate).wait_recv()
    for half in range(2):
        out_ref[:, half * 128 : (half + 1) * 128] = (
            full[half * channels : (half + 1) * channels].astype(jnp.float32) * (1.0 / count)
        )
    taps_ref[...] = full[base:used].astype(jnp.float32) * (1.0 / count)


def tail(product, part, post_relu, conv_input, out_weight, conv_weight, devices, teams):
    total, feat = product.shape
    share_rows = total // teams
    _, _, _, groups, lines, share, _ = part.shape
    tile, width, channels = conv_input.shape
    assert channels == 128 and feat == 256
    size = devices * teams // 2
    used = 11 * channels
    chunk = -(-used // (2 * size * 16)) * 16
    count = float(post_relu.shape[0] * devices)
    vmem = pl.BlockSpec(memory_space=pltpu.VMEM)
    block = (groups, lines, share, feat)
    dma = pltpu.SemaphoreType.DMA
    bf16 = jnp.bfloat16
    return pl.pallas_call(
        lambda *refs: tail_kernel(devices, teams, count, *refs),
        out_shape=(
            jax.ShapeDtypeStruct((PIECES * lines, share, feat), bf16),
            jax.ShapeDtypeStruct((tile, width, channels), bf16),
            jax.ShapeDtypeStruct((channels, feat), jnp.float32),
            jax.ShapeDtypeStruct((9 * channels, channels), jnp.float32),
        ),
        in_specs=[vmem] * 6,
        out_specs=(vmem,) * 4,
        scratch_shapes=[
            pltpu.VMEM((PIECES, 2) + block, bf16),
            pltpu.VMEM((PIECES,) + block, bf16),
            pltpu.VMEM((PIECES,) + block, bf16),
            pltpu.VMEM((teams, share_rows, feat), bf16),
            pltpu.VMEM((PIECES, 2) + block, bf16),
            pltpu.VMEM((PIECES,) + block, bf16),
            pltpu.VMEM((2, width, channels), bf16),
            pltpu.VMEM((2, width, channels), bf16),
            pltpu.VMEM(((tile + 2) * width, channels), jnp.float32),
            pltpu.VMEM(((tile + 2) * width, 3 * channels), bf16),
            pltpu.VMEM((2 * size * chunk, 128), bf16),
            pltpu.VMEM((size * chunk, 128), bf16),
            pltpu.VMEM((size * chunk, 128), bf16),
            pltpu.VMEM((size, chunk, 128), bf16),
            pltpu.VMEM((2 * size * chunk, 128), bf16),
            dma((PIECES,)), dma((PIECES,)), dma((PIECES,)), dma((PIECES,)),
            dma((PIECES, groups)), dma((PIECES, groups)),
            dma((teams,)), dma((teams,)),
            dma((2,)), dma((2,)), dma, dma, dma((size,)), dma((size,)),
            dma((size,)), dma((size,)), dma, dma,
        ],
        compiler_params=pltpu.CompilerParams(
            collective_id=0, has_side_effects=True, vmem_limit_bytes=40 * 2**20
        ),
    )(
        product.reshape(teams, share_rows, feat), part, post_relu, conv_input, out_weight, conv_weight
    )


def body(upstream, centers, post_relu, conv_input, target_feats, out_weight, conv_weight):
    devices = lax.axis_size("src")
    teams = lax.axis_size("tgt")
    product, part = corr_grads(upstream, centers, post_relu, target_feats, out_weight, devices)
    tgt_grad, act_grad, out_wgrad, taps = tail(
        product, part, post_relu, conv_input, out_weight, conv_weight, devices, teams
    )
    return (tgt_grad, act_grad, out_wgrad, taps.reshape(conv_weight.shape))


def solution(mesh):
    placed = (
        P("src", None, None),
        P(None, "src", None),
        P("src", None, None),
        P(("src", "tgt"), None, None),
        P("tgt", None, None),
        P(),
        P(),
    )
    return jax.shard_map(
        body,
        mesh=mesh,
        in_specs=placed,
        out_specs=(P("tgt", "src", None), P(("src", "tgt"), None, None), P(), P()),
        check_vma=False,
    )
```
